1024 devices in a mesh: dp: 64 (over y, z_lo), replica: 16 (over z_hi, x, core).
Axes of the slice: x: 4, y: 4, z: 32 (z_hi: 2, z_lo: 16; z = z_hi * 16 + z_lo), core: 2. Of those that a mesh axis runs over, the one named last changes fastest.
Arguments:
- tokens: bfloat16 [16384, 8, 1152], P(('dp', 'replica')), may hold values from -6 to 6
- token_count: int32 [16384], P(('dp', 'replica')), may hold values from 1 to 8
- image_embed: bfloat16 [16384, 1152], P(('dp', 'replica')), may hold values from -6 to 6
- norm_gain: float32 [1152], replicated, may hold values from 0.25 to 1.75
- head_weight: bfloat16 [1152, 1152], replicated, may hold values from -0.1875 to 0.1875
- head_bias: float32 [1152], replicated, may hold values from -3 to 3
- logit_scale: float32 [1], replicated, may hold values from 1.6 to 2.4
- logit_bias: float32 [1], replicated, may hold values from -8 to -4
Outputs:
- grad_weight: float32 [64, 1152, 1152], P('dp', 'replica')
The draws below stay inside these ranges and needn't reach their ends.
All inputs are finite; a program needn't handle non-finite values.
Results may differ from the reference program's by a relative error of at most 0.019.
Values may be sent and summed in bfloat16 or wider, within the bound.
No kernel may reach another device: no remote copies, remote signals or barrier semaphores. Data moves between devices by JAX's collectives and lax.ppermute only.
A program may use at most 32 MiB of HBM per device.

```python
import jax
import jax.numpy as jnp
from jax import lax

D = 1152
L = 8
B_DEV = 16
CAPTIONS = 16384
N_DP = 64
N_REPLICA = 16


def place_ends(drawn, key, low, top_value):
    longest = drawn.shape.index(max(drawn.shape))
    spots = []
    for shift in (0, 1):
        where = [jax.random.randint(jax.random.fold_in(key, axis), (), 0, length) for axis, length in enumerate(drawn.shape)]
        where[longest] = (where[longest] + shift) % drawn.shape[longest]
        spots.append(tuple(where))
    return drawn.at[spots[0]].set(low).at[spots[1]].set(top_value)


def block_levels(stream_key, dims, pieces, low, largest):
    level = 1.0
    for position, shards_of in pieces:
        draws = jax.random.uniform(jax.random.fold_in(jax.random.fold_in(stream_key, 6), position), (shards_of,), jnp.float32, low / len(pieces), largest / len(pieces))
        level = level * jnp.repeat(jnp.exp(draws), dims[position] // shards_of).reshape((-1,) + (1,) * (len(dims) - 1 - position))
    return level


def gaussian(stream_key, extent, deviation, bound, pieces=(), held_as=jnp.bfloat16):
    entries = jax.random.normal(stream_key, extent, jnp.float32) * deviation
    if len(pieces) > 0:
        entries = block_levels(stream_key, extent, pieces, -0.22, 0.18) * entries
    return jnp.clip(entries, min=-bound, max=bound).astype(held_as)


def setup_inputs(seed: int = 0) -> dict:
    streams_of = jax.random.split(jax.random.key(seed), 9)
    return {
        "tokens": gaussian(streams_of[0], (CAPTIONS, L, D), 1.0, 6.0, ((0, 1024),)),
        "token_count": place_ends(jax.random.randint(streams_of[1], (CAPTIONS,), 1, L + 1), jax.random.fold_in(streams_of[1], 1), 1, L).astype(jnp.int32),
        "image_embed": gaussian(streams_of[2], (CAPTIONS, D), 1.0, 6.0, ((0, 1024),)),
        "norm_gain": jnp.clip(1.0 + 0.15 * jax.random.normal(streams_of[3], (D,), jnp.float32), 0.25, 1.75),
        "head_weight": gaussian(streams_of[4], (D, D), D ** -0.5, 0.1875),
        "head_bias": gaussian(streams_of[5], (D,), 0.5, 3.0, (), jnp.float32),
        "logit_scale": jnp.clip(jax.random.uniform(streams_of[6], (1,), jnp.float32, 1.6, 2.4), 1.6, 2.4),
        "logit_bias": jnp.clip(jax.random.uniform(streams_of[7], (1,), jnp.float32, -8.0, -4.0), -8.0, -4.0),
    }


def gelu_parts(pre):
    coeff = 0.7978845608
    inner = coeff * (pre + 0.044715 * pre * pre * pre)
    hyper = jnp.tanh(inner)
    act = 0.5 * pre * (1.0 + hyper)
    slope = 0.5 * (1.0 + hyper) + 0.5 * pre * (1.0 - hyper * hyper) * coeff * (1.0 + 3.0 * 0.044715 * pre * pre)
    return (act, slope)

def layer_front(tokens, norm_gain, head_weight, head_bias):
    values = tokens.astype(jnp.float32)
    center = lax.optimization_barrier(jnp.mean(values, axis=-1, keepdims=True))
    spread = lax.optimization_barrier(jnp.mean((values - center) ** 2, axis=-1, keepdims=True))
    normed = ((values - center) * lax.rsqrt(spread + 1e-06) * norm_gain).astype(jnp.bfloat16)
    shape = normed.shape
    flat = normed.reshape(-1, shape[-1])
    pre = jnp.dot(flat, head_weight, preferred_element_type=jnp.float32) + head_bias
    return (normed, pre.reshape(shape))

def live_scale(counts, length):
    keep = (jnp.arange(length, dtype=jnp.int32)[None, :] < counts[:, None]).astype(jnp.float32)
    return keep / jnp.maximum(counts, 1).astype(jnp.float32)[:, None]

def reference(tokens, token_count, image_embed, norm_gain, head_weight, head_bias, logit_scale, logit_bias):
    width = D
    length = L
    rows = B_DEV
    helpers = N_REPLICA
    toks = tokens.reshape(N_DP, helpers * rows, length, width)
    counts = token_count.reshape(N_DP, helpers * rows)

    def forward_row(args):
        row_toks, row_counts = args
        normed, pre = layer_front(row_toks, norm_gain, head_weight, head_bias)
        act, slope = gelu_parts(pre)
        scale = live_scale(row_counts, length)
        return lax.optimization_barrier(jnp.sum(act * scale[:, :, None], axis=1))
    pooled = lax.map(forward_row, (toks, counts))
    pooled = pooled.reshape(N_DP, helpers, rows, width)
    size = jnp.sqrt(lax.optimization_barrier(jnp.sum(pooled * pooled, axis=-1, keepdims=True)) + 1e-06)
    unit32 = pooled / size
    unit = unit32.astype(jnp.bfloat16)
    images = image_embed.astype(jnp.float32).reshape(N_DP, helpers, rows, width)
    image = (images / jnp.sqrt(lax.optimization_barrier(jnp.sum(images * images, axis=-1, keepdims=True)) + 1e-06)).astype(jnp.bfloat16)
    temper = jnp.exp(logit_scale[0])
    group = N_DP * rows
    unit_g = jnp.transpose(unit, (1, 0, 2, 3)).reshape(helpers, group, width)
    image_g = jnp.transpose(image, (1, 0, 2, 3)).reshape(helpers, group, width)
    label = jnp.where(jnp.eye(group, dtype=jnp.float32) > 0.5, 1.0, -1.0)

    def group_grad(args):
        unit_r, image_r = args
        cosine = jnp.dot(unit_r, image_r.T, preferred_element_type=jnp.float32)
        logit = temper * cosine + logit_bias[0]
        dlogit = (-label / (1.0 + jnp.exp(label * logit)) / group).astype(jnp.bfloat16)
        return temper * jnp.dot(dlogit, image_r, preferred_element_type=jnp.float32)
    dunit = lax.map(group_grad, (unit_g, image_g))
    dunit = jnp.transpose(dunit.reshape(helpers, N_DP, rows, width), (1, 0, 2, 3))
    dpooled = (dunit - unit32 * lax.optimization_barrier(jnp.sum(unit32 * dunit, axis=-1, keepdims=True))) / size
    dpooled = dpooled.reshape(N_DP, helpers * rows, width)

    def backward_row(args):
        row_toks, row_counts, row_dpooled = args
        normed, pre = layer_front(row_toks, norm_gain, head_weight, head_bias)
        act, slope = gelu_parts(pre)
        scale = live_scale(row_counts, length)
        dpre = (row_dpooled[:, None, :] * scale[:, :, None] * slope).astype(jnp.bfloat16)
        left = normed.reshape(-1, width)
        right = dpre.reshape(-1, width)
        return lax.dot_general(left, right, (((0,), (0,)), ((), ())), preferred_element_type=jnp.float32)
    return lax.map(backward_row, (toks, counts, dpooled))
```

```python
import jax
import jax.numpy as jnp
from jax import lax
from jax.sharding import Mesh, PartitionSpec as P

AXES = ("y", "za", "zb", "zh", "x", "c")
SIZES = (4, 4, 4, 2, 4, 2)


def gelu_terms(pre):
    coeff = 0.7978845608
    inner = coeff * (pre + 0.044715 * pre * pre * pre)
    return coeff, jnp.tanh(inner)


def gelu(pre):
    _, hyper = gelu_terms(pre)
    return 0.5 * pre * (1.0 + hyper)


def gelu_slope(pre):
    coeff, hyper = gelu_terms(pre)
    return 0.5 * (1.0 + hyper) + 0.5 * pre * (1.0 - hyper * hyper) * coeff * (
        1.0 + 3.0 * 0.044715 * pre * pre
    )


def spread_to(value, axes, count):
    copies = jnp.broadcast_to(value[None], (count,) + value.shape)
    return lax.all_to_all(copies, axes, split_axis=0, concat_axis=0, tiled=True)


def on_device(
    tokens, token_count, image_embed, norm_gain, head_weight, head_bias, logit_scale, logit_bias
):
    rows, length, width = tokens.shape
    part = width // 16
    group = 64 * rows
    my = {name: lax.axis_index(name) for name in AXES}

    images = image_embed.astype(jnp.float32)
    image = (images / jnp.sqrt(jnp.sum(images * images, axis=-1, keepdims=True) + 1e-06)).astype(
        jnp.bfloat16
    )
    some_images = spread_to(image, "za", 4).reshape(4 * rows, width)

    values = tokens.reshape(rows * length, width).astype(jnp.float32)
    center = jnp.mean(values, axis=-1, keepdims=True)
    spread = jnp.mean((values - center) ** 2, axis=-1, keepdims=True)
    normed = ((values - center) * lax.rsqrt(spread + 1e-06) * norm_gain).astype(jnp.bfloat16)
    live = jnp.arange(length, dtype=jnp.int32) < token_count[:, None]
    live_flat = live.reshape(rows * length, 1)
    masked = jnp.where(live_flat, normed, 0)

    by_x = spread_to(masked, "x", 4)
    other = lax.ppermute(by_x, "c", [(0, 1), (1, 0)])

    pre = jnp.dot(normed, head_weight, preferred_element_type=jnp.float32) + head_bias
    per_count = 1.0 / token_count.astype(jnp.float32)[:, None]
    scale = live.astype(jnp.float32) * per_count
    pooled = jnp.sum(gelu(pre).reshape(rows, length, width) * scale[:, :, None], axis=1)
    size = jnp.sqrt(jnp.sum(pooled * pooled, axis=-1, keepdims=True) + 1e-06)
    unit32 = pooled / size
    unit = unit32.astype(jnp.bfloat16)
    units = spread_to(unit, ("y", "zb"), 16).reshape(16 * rows, width)

    temper = jnp.exp(logit_scale[0])
    cosine = jnp.dot(units, some_images.T, preferred_element_type=jnp.float32)
    logit = temper * cosine + logit_bias[0]
    unit_at = lax.broadcasted_iota(jnp.int32, cosine.shape, 0)
    image_at = lax.broadcasted_iota(jnp.int32, cosine.shape, 1)
    same = (unit_at - (my["y"] * 4 + my["zb"]) * rows) == (image_at - my["za"] * rows)
    mine = (unit_at // rows) == (my["y"] * 4 + my["zb"])
    label = jnp.where(same & mine, 1.0, -1.0)
    dlogit = (-label / (1.0 + jnp.exp(label * logit)) / group).astype(jnp.bfloat16)
    terms = jnp.dot(dlogit, some_images, preferred_element_type=jnp.float32).astype(jnp.bfloat16)
    terms = lax.all_to_all(
        terms.reshape(16, rows, width), ("y", "zb"), split_axis=0, concat_axis=0, tiled=True
    )
    dunit = temper * jnp.sum(terms.astype(jnp.float32), axis=0)
    dpooled = (dunit - unit32 * jnp.sum(unit32 * dunit, axis=-1, keepdims=True)) / size
    share = (dpooled * per_count).astype(jnp.bfloat16)
    shares = spread_to(share, ("x", "c"), 8)

    first = my["c"] == 0
    halves = jnp.stack(
        [jnp.where(first, by_x, other), jnp.where(first, other, by_x)], axis=1
    ).reshape(8 * rows * length, width)
    slope = gelu_slope(
        jnp.dot(halves, head_weight, preferred_element_type=jnp.float32) + head_bias
    ).astype(jnp.bfloat16)
    here = my["x"] * 2 + my["c"]
    wanted = lax.broadcasted_iota(jnp.int32, (width, 2 * part), 1)
    source = lax.broadcasted_iota(jnp.int32, (width, 2 * part), 0)
    half_of = wanted // part
    zh_of = jnp.where(half_of == 0, my["zh"], 1 - my["zh"])
    pick = (source == (zh_of * 8 + here) * part + wanted % part).astype(jnp.bfloat16)
    columns = jnp.dot(halves, pick, preferred_element_type=jnp.float32).astype(jnp.bfloat16)
    slope, columns = lax.optimization_barrier((slope, columns))

    dpre = (
        shares.reshape(8 * rows, 1, width).astype(jnp.float32)
        * slope.reshape(8 * rows, length, width).astype(jnp.float32)
    ).astype(jnp.bfloat16)
    both = lax.dot_general(
        columns,
        dpre.reshape(8 * rows * length, width),
        (((0,), (0,)), ((), ())),
        preferred_element_type=jnp.float32,
    )
    away = lax.ppermute(both[part:].astype(jnp.bfloat16), "zh", [(0, 1), (1, 0)])
    return (both[:part] + away.astype(jnp.float32))[None]


def solution(mesh):
    fine = Mesh(mesh.devices.reshape(SIZES), AXES)
    everyone = AXES
    in_specs = (
        P(everyone, None, None),
        P(everyone),
        P(everyone, None),
        P(),
        P(),
        P(),
        P(),
        P(),
    )
    out_specs = P(("y", "za", "zb"), ("zh", "x", "c"), None)
    return jax.shard_map(
        on_device, mesh=fine, in_specs=in_specs, out_specs=out_specs, check_vma=False
    )
```

```python
import jax
import jax.numpy as jnp
from jax import lax
from jax.sharding import Mesh, PartitionSpec as P

AXES = ("y", "za", "zb", "zh", "x", "c")
SIZES = (4, 4, 4, 2, 4, 2)


def size_of(*names):
    count = 1
    for name in names:
        count *= SIZES[AXES.index(name)]
    return count


def gelu_terms(pre):
    coeff = 0.7978845608
    inner = coeff * (pre + 0.044715 * pre * pre * pre)
    return coeff, jnp.tanh(inner)


def gelu(pre):
    _, hyper = gelu_terms(pre)
    return 0.5 * pre * (1.0 + hyper)


def gelu_slope(pre):
    coeff, hyper = gelu_terms(pre)
    return 0.5 * (1.0 + hyper) + 0.5 * pre * (1.0 - hyper * hyper) * coeff * (
        1.0 + 3.0 * 0.044715 * pre * pre
    )


def spread_to(value, *axes):
    copies = jnp.broadcast_to(value[None], (size_of(*axes),) + value.shape)
    return lax.all_to_all(copies, axes, split_axis=0, concat_axis=0, tiled=True)


def from_others(value, axis):
    count = size_of(axis)
    moved = [
        lax.ppermute(value, axis, [(i, (i + k) % count) for i in range(count)])
        for k in range(1, count)
    ]
    return [value] + moved


def on_device(
    tokens, token_count, image_embed, norm_gain, head_weight, head_bias, logit_scale, logit_bias
):
    rows, length, width = tokens.shape
    part = width // size_of("zh", "x", "c")
    group = size_of("y", "za", "zb") * rows
    my = {name: lax.axis_index(name) for name in AXES}

    images = image_embed.astype(jnp.float32)
    image = (images / jnp.sqrt(jnp.sum(images * images, axis=-1, keepdims=True) + 1e-06)).astype(
        jnp.bfloat16
    )
    tokens, image = lax.optimization_barrier((tokens, image))
    some_images = spread_to(image, "za").reshape(-1, width)

    values = tokens.reshape(rows * length, width).astype(jnp.float32)
    center = jnp.mean(values, axis=-1, keepdims=True)
    spread = jnp.mean((values - center) ** 2, axis=-1, keepdims=True)
    normed = ((values - center) * lax.rsqrt(spread + 1e-06) * norm_gain).astype(jnp.bfloat16)
    live = jnp.arange(length, dtype=jnp.int32) < token_count[:, None]
    masked = jnp.where(live.reshape(rows * length, 1), normed, 0)

    pre = jnp.dot(normed, head_weight, preferred_element_type=jnp.float32) + head_bias
    per_count = 1.0 / token_count.astype(jnp.float32)[:, None]
    scale = live.astype(jnp.float32) * per_count
    pooled = jnp.sum(gelu(pre).reshape(rows, length, width) * scale[:, :, None], axis=1)
    size = jnp.sqrt(jnp.sum(pooled * pooled, axis=-1, keepdims=True) + 1e-06)
    unit32 = pooled / size
    unit = unit32.astype(jnp.bfloat16)
    units = from_others(unit, "zb")
    masked, units = lax.optimization_barrier((masked, units))
    by_x = jnp.concatenate(from_others(masked, "x"))
    other = lax.ppermute(by_x, "c", [(0, 1), (1, 0)])

    units, some_images = lax.optimization_barrier((units, some_images))
    units = jnp.concatenate(units)
    all_images = spread_to(some_images, "y").reshape(-1, width)

    temper = jnp.exp(logit_scale[0])
    cosine = jnp.dot(units, all_images.T, preferred_element_type=jnp.float32)
    logit = temper * cosine + logit_bias[0]
    unit_at = lax.broadcasted_iota(jnp.int32, cosine.shape, 0)
    image_at = lax.broadcasted_iota(jnp.int32, cosine.shape, 1)
    same = unit_at == image_at - (my["y"] * size_of("za") + my["za"]) * rows
    label = jnp.where(same & (unit_at < rows), 1.0, -1.0)
    dlogit = (-label / (1.0 + jnp.exp(label * logit)) / group).astype(jnp.bfloat16)
    terms = jnp.dot(dlogit, all_images, preferred_element_type=jnp.float32).astype(jnp.bfloat16)
    near = size_of("zb")
    return_to = (my["zb"] - jnp.arange(near)) % near
    terms = terms.reshape(near, rows, width)[return_to]
    terms, other = lax.optimization_barrier((terms, other))
    halves = jnp.concatenate([by_x, other])
    terms = lax.all_to_all(terms, "zb", split_axis=0, concat_axis=0, tiled=True)
    dunit = temper * jnp.sum(terms.astype(jnp.float32), axis=0)
    dpooled = (dunit - unit32 * jnp.sum(unit32 * dunit, axis=-1, keepdims=True)) / size
    share = (dpooled * per_count).astype(jnp.bfloat16)
    slope = gelu_slope(
        jnp.dot(halves, head_weight, preferred_element_type=jnp.float32) + head_bias
    ).astype(jnp.bfloat16)
    here = my["x"] * 2 + my["c"]
    team = 2 * size_of("x")
    wanted = lax.broadcasted_iota(jnp.int32, (width, 2 * part), 1)
    source = lax.broadcasted_iota(jnp.int32, (width, 2 * part), 0)
    half_of = wanted // part
    zh_of = jnp.where(half_of == 0, my["zh"], 1 - my["zh"])
    pick = (source == (zh_of * team + here) * part + wanted % part).astype(jnp.bfloat16)
    columns = jnp.dot(halves, pick, preferred_element_type=jnp.float32).astype(jnp.bfloat16)
    share, slope, columns = lax.optimization_barrier((share, slope, columns))
    shares = spread_to(share, "x", "c")
    along = size_of("x")
    owners = jnp.stack(
        [((my["x"] - k) % along) * 2 + (my["c"] ^ j) for j in (0, 1) for k in range(along)]
    )
    shares = shares[owners]

    dpre = (
        shares.reshape(team * rows, 1, width).astype(jnp.float32)
        * slope.reshape(team * rows, length, width).astype(jnp.float32)
    ).astype(jnp.bfloat16)
    both = lax.dot_general(
        columns,
        dpre.reshape(team * rows * length, width),
        (((0,), (0,)), ((), ())),
        preferred_element_type=jnp.float32,
    )
    away = lax.ppermute(both[part:].astype(jnp.bfloat16), "zh", [(0, 1), (1, 0)])
    return (both[:part] + away.astype(jnp.float32))[None]


def solution(mesh):
    fine = Mesh(mesh.devices.reshape(SIZES), AXES)
    everyone = AXES
    in_specs = (
        P(everyone, None, None),
        P(everyone),
        P(everyone, None),
        P(),
        P(),
        P(),
        P(),
        P(),
    )
    out_specs = P(("y", "za", "zb"), ("zh", "x", "c"), None)
    return jax.shard_map(
        on_device, mesh=fine, in_specs=in_specs, out_specs=out_specs, check_vma=False
    )
```

```python
import functools

import jax
import jax.numpy as jnp
from jax import lax
from jax.experimental import pallas as pl
from jax.experimental.pallas import tpu as pltpu
from jax.sharding import Mesh, PartitionSpec as P

AXES = ("y", "za", "zb", "zh", "x", "c")
SIZES = (4, 4, 4, 2, 4, 2)
COEFF = 0.7978845608
CUBIC = 0.044715
BF16, F32 = jnp.bfloat16, jnp.float32


def size_of(*names):
    count = 1
    for name in names:
        count *= SIZES[AXES.index(name)]
    return count


def from_others(value, axis):
    count = size_of(axis)
    moved = [
        lax.ppermute(value, axis, [(i, (i + k) % count) for i in range(count)])
        for k in range(1, count)
    ]
    return [value] + moved


def exchange(copies, *axes):
    return lax.all_to_all(copies, axes, split_axis=0, concat_axis=0, tiled=True)


def local(body, outs, *args, smem=(), scratch=(), flops=0, moved=0):
    vmem = pl.BlockSpec(memory_space=pltpu.VMEM)
    in_specs = [pl.BlockSpec(memory_space=pltpu.SMEM) if i in smem else vmem for i in range(len(args))]
    return pl.pallas_call(
        body,
        out_shape=[jax.ShapeDtypeStruct(shape, dtype) for shape, dtype in outs],
        in_specs=in_specs,
        out_specs=[vmem] * len(outs),
        scratch_shapes=[pltpu.VMEM(shape, dtype) for shape, dtype in scratch],
        compiler_params=pltpu.CompilerParams(vmem_limit_bytes=40 * 1024 * 1024),
        cost_estimate=pl.CostEstimate(flops=flops, bytes_accessed=moved, transcendentals=0),
    )(*args)


def image_kernel(image_ref, out_ref):
    images = image_ref[...].astype(F32)
    norm = jnp.sqrt(jnp.sum(images * images, axis=-1, keepdims=True) + 1e-06)
    image = (images / norm).astype(BF16)
    for k in range(out_ref.shape[0]):
        out_ref[k] = image


def front_kernel(
    count_ref, token_ref, gain_ref, weight_ref, bias_ref, masked_ref, unit_ref, pooled_ref, share_ref, act_ref
):
    rows, width = pooled_ref.shape
    length = token_ref.shape[0] // rows
    values = token_ref[...].astype(F32)
    center = jnp.mean(values, axis=-1, keepdims=True)
    spread = jnp.mean((values - center) ** 2, axis=-1, keepdims=True)
    gain = gain_ref[...].reshape(1, width)
    normed = ((values - center) * lax.rsqrt(spread + 1e-06) * gain).astype(BF16)
    pre = jnp.dot(normed, weight_ref[...], preferred_element_type=F32)
    pre = pre + bias_ref[...].reshape(1, width)
    act_ref[...] = 0.5 * pre * (1.0 + jnp.tanh(COEFF * (pre + CUBIC * pre * pre * pre)))
    slot = lax.broadcasted_iota(jnp.int32, (length, 1), 0)
    lives = []
    for p in range(rows):
        live = (slot < count_ref[p]).astype(F32)
        inverse = 1.0 / jnp.full((length, 1), count_ref[p], jnp.int32).astype(F32)
        part = act_ref[p * length : (p + 1) * length, :] * (live * inverse)
        pooled_ref[p : p + 1, :] = jnp.sum(part, axis=0, keepdims=True)
        share_ref[p : p + 1, :] = jnp.broadcast_to(inverse[:1], (1, share_ref.shape[1]))
        lives.append(live)
    masked_ref[...] = normed * jnp.concatenate(lives, axis=0).astype(BF16)
    pooled = pooled_ref[...]
    size = jnp.sqrt(jnp.sum(pooled * pooled, axis=-1, keepdims=True) + 1e-06)
    unit_ref[...] = (pooled / size).astype(BF16)


def stack_kernel(*refs):
    *piece_refs, out_ref = refs
    block = piece_refs[0].shape[0]
    for k, ref in enumerate(piece_refs):
        out_ref[k * block : (k + 1) * block, :] = ref[...]


def copies_kernel(image_ref, out_ref):
    for k in range(out_ref.shape[0]):
        for j in range(image_ref.shape[0]):
            rows = image_ref.shape[1]
            out_ref[k, j * rows : (j + 1) * rows, :] = image_ref[j]


def logit_kernel(scale_ref, shift_ref, *refs):
    *unit_refs, image_ref, out_ref = refs
    near, rows, width = out_ref.shape
    group = rows * size_of("y", "za", "zb")
    units = jnp.concatenate([ref[...] for ref in unit_refs], axis=0)
    images = image_ref[...]
    temper = jnp.exp(jnp.full((1, 1), scale_ref[0], F32))
    cosine = lax.dot_general(units, images, (((1,), (1,)), ((), ())), preferred_element_type=F32)
    logit = temper * cosine + shift_ref[0]
    unit_at = lax.broadcasted_iota(jnp.int32, cosine.shape, 0)
    image_at = lax.broadcasted_iota(jnp.int32, cosine.shape, 1)
    offset = (lax.axis_index("y") * size_of("za") + lax.axis_index("za")) * rows
    label = jnp.where((unit_at == image_at - offset) & (unit_at < rows), 1.0, -1.0)
    dlogit = (-label / (1.0 + jnp.exp(label * logit)) / group).astype(BF16)
    terms = jnp.dot(dlogit, images, preferred_element_type=F32).astype(BF16)
    for k in range(near):
        owner = lax.rem(lax.axis_index("zb") + near - k, near)
        out_ref[owner] = terms[k * rows : (k + 1) * rows]


def share_kernel(scale_ref, term_ref, pooled_ref, inverse_ref, out_ref):
    temper = jnp.exp(jnp.full((1, 1), scale_ref[0], F32))
    pooled = pooled_ref[...]
    size = jnp.sqrt(jnp.sum(pooled * pooled, axis=-1, keepdims=True) + 1e-06)
    unit = pooled / size
    total = term_ref[0].astype(F32)
    for k in range(1, term_ref.shape[0]):
        total = total + term_ref[k].astype(F32)
    dunit = temper * total
    dpooled = (dunit - unit * jnp.sum(unit * dunit, axis=-1, keepdims=True)) / size
    share = (dpooled * inverse_ref[:, :1]).astype(BF16)
    for k in range(out_ref.shape[0]):
        out_ref[k] = share


def slope_kernel(weight_ref, bias_ref, *refs):
    *piece_refs, first_ref, second_ref, column_ref = refs
    width = weight_ref.shape[0]
    block = piece_refs[0].shape[0]
    part = column_ref.shape[0] // 2
    split = first_ref.shape[1]
    here = lax.axis_index("x") * size_of("c") + lax.axis_index("c")
    team = size_of("x", "c")
    half = lax.axis_index("zh")
    row = lax.broadcasted_iota(jnp.int32, (2 * part, width), 0)
    source = lax.broadcasted_iota(jnp.int32, (2 * part, width), 1)
    near = (half * team + here) * part
    far = ((1 - half) * team + here) * part - part
    pick = jnp.where(source == row + jnp.where(row < part, near, far), 1.0, 0.0).astype(BF16)
    bias = bias_ref[...].reshape(1, width)
    at = 0
    for ref in piece_refs:
        for begin in range(0, ref.shape[0], block):
            piece = ref[begin : begin + block, :]
            pre = jnp.dot(piece, weight_ref[...], preferred_element_type=F32) + bias
            square = pre * pre
            hyper = jnp.tanh(COEFF * (pre + CUBIC * pre * square))
            slope = 0.5 * (1.0 + hyper) + 0.5 * pre * (1.0 - hyper * hyper) * COEFF * (
                1.0 + 3.0 * CUBIC * square
            )
            slope = slope.astype(BF16)
            first_ref[at : at + block, :] = slope[:, :split]
            second_ref[at : at + block, :] = slope[:, split:]
            columns = lax.dot_general(
                pick, piece, (((1,), (1,)), ((), ())), preferred_element_type=F32
            )
            column_ref[:, at : at + block] = columns.astype(BF16)
            at += block


def grad_kernel(begin, share_ref, slope_ref, column_ref, far_ref, near_ref, dpre_ref):
    team, rows, _ = share_ref.shape
    total, cols = slope_ref.shape
    block = total // team
    along, cores = size_of("x"), size_of("c")
    part = near_ref.shape[0]
    x, c = lax.axis_index("x"), lax.axis_index("c")
    for j in range(cores):
        for k in range(along):
            at = (j * along + k) * block
            owner = lax.rem(x + along - k, along) * cores + lax.rem(c + j, cores)
            share = share_ref[owner, :, begin : begin + cols].astype(F32)
            share = jnp.broadcast_to(share[:, None, :], (rows, block // rows, cols)).reshape(block, cols)
            slope = slope_ref[at : at + block, :].astype(F32)
            dpre_ref[at : at + block, :] = (share * slope).astype(BF16)
    both = jnp.dot(column_ref[...], dpre_ref[...], preferred_element_type=F32)
    near_ref[...] = both[:part]
    far_ref[...] = both[part:].astype(BF16)


def add_kernel(near1_ref, near2_ref, away1_ref, away2_ref, out_ref):
    split = near1_ref.shape[1]
    out_ref[0, :, :split] = near1_ref[...] + away1_ref[...].astype(F32)
    out_ref[0, :, split:] = near2_ref[...] + away2_ref[...].astype(F32)


def on_device(
    tokens, token_count, image_embed, norm_gain, head_weight, head_bias, logit_scale, logit_bias
):
    rows, length, width = tokens.shape
    part = width // size_of("zh", "x", "c")
    team = size_of("x", "c")
    flat = rows * length
    total = team * flat
    split = (width // 2 + 127) // 128 * 128
    swap = [(0, 1), (1, 0)]

    (image,) = local(image_kernel, [((size_of("za"), rows, width), BF16)], image_embed)
    tokens, image = lax.optimization_barrier((tokens, image))
    some_images = exchange(image, "za")

    masked, unit, pooled, inverse = local(
        front_kernel,
        [((flat, width), BF16), ((rows, width), BF16), ((rows, width), F32), ((rows, 128), F32)],
        token_count,
        tokens.reshape(flat, width),
        norm_gain,
        head_weight,
        head_bias,
        smem=(0,),
        scratch=[((flat, width), F32)],
        flops=2 * flat * width * width,
        moved=2 * width * width,
    )
    units = from_others(unit, "zb")
    masked, units = lax.optimization_barrier((masked, units))
    by_x = from_others(masked, "x")
    by_x, units, some_images = lax.optimization_barrier((by_x, units, some_images))
    (copies,) = local(
        copies_kernel, [((size_of("y"), size_of("za") * rows, width), BF16)], some_images
    )
    (stacked,) = local(stack_kernel, [((size_of("x") * flat, width), BF16)], *by_x)
    other = lax.ppermute(stacked, "c", swap)
    all_images = exchange(copies, "y").reshape(-1, width)
    (terms,) = local(
        logit_kernel,
        [((size_of("zb"), rows, width), BF16)],
        logit_scale,
        logit_bias,
        *units,
        all_images,
        smem=(0, 1),
    )
    terms, other = lax.optimization_barrier((terms, other))
    terms = exchange(terms, "zb")
    first, second, columns = local(
        slope_kernel,
        [((total, split), BF16), ((total, width - split), BF16), ((2 * part, total), BF16)],
        head_weight,
        head_bias,
        *by_x,
        other,
        flops=2 * total * width * width,
        moved=2 * width * width + 4 * total * width,
    )
    (share,) = local(
        share_kernel,
        [((team, rows, width), BF16)],
        logit_scale,
        terms,
        pooled,
        inverse,
        smem=(0,),
    )
    share, first, second, columns = lax.optimization_barrier((share, first, second, columns))
    shares = exchange(share, "x", "c")
    away, near = [], []
    for begin, slope in ((0, first), (split, second)):
        cols = slope.shape[1]
        far, mine = local(
            functools.partial(grad_kernel, begin),
            [((part, cols), BF16), ((part, cols), F32)],
            shares,
            slope,
            columns,
            scratch=[((total, cols), BF16)],
            flops=4 * part * total * cols,
            moved=2 * total * cols,
        )
        away.append(lax.ppermute(far, "zh", swap))
        near.append(mine)
    (grad,) = local(add_kernel, [((1, part, width), F32)], *near, *away)
    return grad


def solution(mesh):
    fine = Mesh(mesh.devices.reshape(SIZES), AXES)
    in_specs = (
        P(AXES, None, None),
        P(AXES),
        P(AXES, None),
        P(),
        P(),
        P(),
        P(),
        P(),
    )
    out_specs = P(("y", "za", "zb"), ("zh", "x", "c"), None)
    return jax.shard_map(
        on_device, mesh=fine, in_specs=in_specs, out_specs=out_specs, check_vma=False
    )
```

```python
import jax
import jax.numpy as jnp
from jax import lax
from jax.experimental import pallas as pl
from jax.experimental.pallas import tpu as pltpu
from jax.sharding import Mesh, PartitionSpec as P

AXES = ("y", "za", "zb", "zh", "x", "c")
SIZES = (4, 4, 4, 2, 4, 2)
VMEM_LIMIT = 60 * 1024 * 1024
COEFF = 0.7978845608
CUBIC = 0.044715
BF16, F32 = jnp.bfloat16, jnp.float32


def size_of(*names):
    count = 1
    for name in names:
        count *= SIZES[AXES.index(name)]
    return count


def from_others(value, axis):
    count = size_of(axis)
    moved = [
        lax.ppermute(value, axis, [(i, (i + k) % count) for i in range(count)])
        for k in range(1, count)
    ]
    return [value] + moved


def exchange(copies, *axes):
    return lax.all_to_all(copies, axes, split_axis=0, concat_axis=0, tiled=True)


def local(body, outs, *args, smem=(), scratch=(), flops=0, moved=0):
    def whole(shape, space):
        return pl.BlockSpec(shape, lambda i: (0,) * len(shape), memory_space=space)

    return pl.pallas_call(
        body,
        grid=(1,),
        out_shape=[jax.ShapeDtypeStruct(shape, dtype) for shape, dtype in outs],
        in_specs=[whole(v.shape, pltpu.SMEM if i in smem else None) for i, v in enumerate(args)],
        out_specs=[whole(shape, None) for shape, _ in outs],
        scratch_shapes=[pltpu.VMEM(shape, dtype) for shape, dtype in scratch],
        compiler_params=pltpu.CompilerParams(vmem_limit_bytes=VMEM_LIMIT),
        cost_estimate=pl.CostEstimate(flops=flops, bytes_accessed=moved, transcendentals=0),
    )(*args)


def first_kernel(count_ref, image_ref, token_ref, copies_ref, live_ref):
    images = image_ref[...].astype(F32)
    norm = jnp.sqrt(jnp.sum(images * images, axis=-1, keepdims=True) + 1e-06)
    image = (images / norm).astype(BF16)
    for k in range(copies_ref.shape[0]):
        copies_ref[k] = image
    rows = image_ref.shape[0]
    length = token_ref.shape[0] // rows
    slot = lax.broadcasted_iota(jnp.int32, (length, 1), 0)
    lives = [(slot < count_ref[p]).astype(F32) for p in range(rows)]
    live_ref[...] = token_ref[...] * jnp.concatenate(lives, axis=0).astype(BF16)


def layer(token_ref, gain_ref, weight_ref, bias_ref, slope_ref, column_ref):
    width = token_ref.shape[1]
    values = token_ref[...].astype(F32)
    center = jnp.mean(values, axis=-1, keepdims=True)
    spread = jnp.mean((values - center) ** 2, axis=-1, keepdims=True)
    gain = gain_ref[...].reshape(1, width)
    normed = ((values - center) * lax.rsqrt(spread + 1e-06) * gain).astype(BF16)
    pre = jnp.dot(normed, weight_ref[...], preferred_element_type=F32)
    pre = pre + bias_ref[...].reshape(1, width)
    square = pre * pre
    hyper = jnp.tanh(COEFF * (pre + CUBIC * pre * square))
    slope = 0.5 * (1.0 + hyper) + 0.5 * pre * (1.0 - hyper * hyper) * COEFF * (
        1.0 + 3.0 * CUBIC * square
    )
    slope_ref[...] = slope.astype(BF16)
    half, cores = column_ref.shape[0], size_of("c")
    part = half // size_of("x", "c")
    row = lax.broadcasted_iota(jnp.int32, (half, width), 0)
    source = lax.broadcasted_iota(jnp.int32, (half, width), 1) - lax.axis_index("zh") * half
    core = lax.axis_index("c")
    rest = half // cores
    mine = row < rest
    place = jnp.where(mine, row, row - rest)
    group = place * 0
    for k in range(1, size_of("x")):
        group = group + jnp.where(place >= k * part, 1, 0)
    wanted = (group * cores + jnp.where(mine, core, 1 - core)) * part + place - group * part
    pick = jnp.where(source == wanted, 1.0, 0.0).astype(BF16)
    columns = lax.dot_general(pick, normed, (((1,), (1,)), ((), ())), preferred_element_type=F32)
    column_ref[...] = columns.astype(BF16)
    return 0.5 * pre * (1.0 + hyper)


def front_kernel(
    count_ref, token_ref, gain_ref, weight_ref, bias_ref,
    unit_ref, pooled_ref, inverse_ref, slope_ref, column_ref, act_ref,
):
    rows = pooled_ref.shape[0]
    length = token_ref.shape[0] // rows
    act_ref[...] = layer(token_ref, gain_ref, weight_ref, bias_ref, slope_ref, column_ref)
    slot = lax.broadcasted_iota(jnp.int32, (length, 1), 0)
    for p in range(rows):
        live = (slot < count_ref[p]).astype(F32)
        inverse = 1.0 / jnp.full((length, 1), count_ref[p], jnp.int32).astype(F32)
        part = act_ref[p * length : (p + 1) * length, :] * (live * inverse)
        pooled_ref[p : p + 1, :] = jnp.sum(part, axis=0, keepdims=True)
        inverse_ref[p : p + 1, :] = jnp.broadcast_to(inverse[:1], (1, inverse_ref.shape[1]))
    pooled = pooled_ref[...]
    size = jnp.sqrt(jnp.sum(pooled * pooled, axis=-1, keepdims=True) + 1e-06)
    unit_ref[...] = (pooled / size).astype(BF16)


def partner_kernel(token_ref, gain_ref, weight_ref, bias_ref, slope_ref, column_ref):
    layer(token_ref, gain_ref, weight_ref, bias_ref, slope_ref, column_ref)


def copies_kernel(image_ref, out_ref):
    rows = image_ref.shape[1]
    for k in range(out_ref.shape[0]):
        for j in range(image_ref.shape[0]):
            out_ref[k, j * rows : (j + 1) * rows, :] = image_ref[j]


def logit_kernel(scale_ref, shift_ref, *refs):
    *unit_refs, image_ref, out_ref = refs
    near, rows, width = out_ref.shape
    group = rows * size_of("y", "za", "zb")
    units = jnp.concatenate([ref[...] for ref in unit_refs], axis=0)
    images = image_ref[...]
    temper = jnp.exp(jnp.full((1, 1), scale_ref[0], F32))
    cosine = lax.dot_general(units, images, (((1,), (1,)), ((), ())), preferred_element_type=F32)
    logit = temper * cosine + shift_ref[0]
    unit_at = lax.broadcasted_iota(jnp.int32, cosine.shape, 0)
    image_at = lax.broadcasted_iota(jnp.int32, cosine.shape, 1)
    offset = (lax.axis_index("y") * size_of("za") + lax.axis_index("za")) * rows
    label = jnp.where((unit_at == image_at - offset) & (unit_at < rows), 1.0, -1.0)
    dlogit = (-label / (1.0 + jnp.exp(label * logit)) / group).astype(BF16)
    terms = jnp.dot(dlogit, images, preferred_element_type=F32).astype(BF16)
    for k in range(near):
        owner = lax.rem(lax.axis_index("zb") + near - k, near)
        out_ref[owner] = terms[k * rows : (k + 1) * rows]


def share_kernel(scale_ref, term_ref, pooled_ref, inverse_ref, out_ref):
    temper = jnp.exp(jnp.full((1, 1), scale_ref[0], F32))
    pooled = pooled_ref[...]
    size = jnp.sqrt(jnp.sum(pooled * pooled, axis=-1, keepdims=True) + 1e-06)
    unit = pooled / size
    total = term_ref[0].astype(F32)
    for k in range(1, term_ref.shape[0]):
        total = total + term_ref[k].astype(F32)
    dunit = temper * total
    dpooled = (dunit - unit * jnp.sum(unit * dunit, axis=-1, keepdims=True)) / size
    out_ref[...] = (dpooled * inverse_ref[:, :1]).astype(BF16)


def grad_kernel(*refs):
    *in_refs, keep_ref, send_ref = refs
    rest = keep_ref.shape[0]
    total = None
    for share_ref, slope_ref, column_ref in (in_refs[:3], in_refs[3:]):
        rows, width = share_ref.shape
        flat = slope_ref.shape[0]
        share = share_ref[...].astype(F32)
        share = jnp.broadcast_to(share[:, None, :], (rows, flat // rows, width)).reshape(flat, width)
        dpre = (share * slope_ref[...].astype(F32)).astype(BF16)
        grad = jnp.dot(column_ref[...], dpre, preferred_element_type=F32)
        total = grad if total is None else total + grad
    keep_ref[...] = total[:rest]
    send_ref[...] = total[rest:].astype(BF16)


def core_kernel(keep_ref, away_ref, out_ref):
    total = keep_ref[...] + away_ref[...].astype(F32)
    part = out_ref.shape[1]
    for k in range(out_ref.shape[0]):
        out_ref[k] = total[k * part : (k + 1) * part].astype(BF16)


def sum_kernel(in_ref, out_ref):
    total = in_ref[0].astype(F32)
    for k in range(1, in_ref.shape[0]):
        total = total + in_ref[k].astype(F32)
    out_ref[0] = total


def on_device(
    tokens, token_count, image_embed, norm_gain, head_weight, head_bias, logit_scale, logit_bias
):
    rows, length, width = tokens.shape
    part = width // size_of("zh", "x", "c")
    flat = rows * length
    half = width // 2
    swap = [(0, 1), (1, 0)]

    image, alive = local(
        first_kernel,
        [((size_of("za"), rows, width), BF16), ((flat, width), BF16)],
        token_count,
        image_embed,
        tokens.reshape(flat, width),
        smem=(0,),
    )
    partner = lax.ppermute(alive, "zh", swap)

    def own(image, alive, norm_gain, head_weight, head_bias):
        some_images = exchange(image, "za")
        unit, pooled, inverse, slope, columns = local(
            front_kernel,
            [
                ((rows, width), BF16),
                ((rows, width), F32),
                ((rows, 128), F32),
                ((flat, width), BF16),
                ((half, flat), BF16),
            ],
            token_count,
            alive,
            norm_gain,
            head_weight,
            head_bias,
            smem=(0,),
            scratch=[((flat, width), F32)],
            flops=2 * flat * width * width,
            moved=2 * width * width,
        )
        units = from_others(unit, "zb")
        units, some_images = lax.optimization_barrier((units, some_images))
        (copies,) = local(
            copies_kernel, [((size_of("y"), size_of("za") * rows, width), BF16)], some_images
        )
        all_images = exchange(copies, "y").reshape(-1, width)
        (terms,) = local(
            logit_kernel,
            [((size_of("zb"), rows, width), BF16)],
            logit_scale,
            logit_bias,
            *units,
            all_images,
            smem=(0, 1),
        )
        terms = exchange(terms, "zb")
        (share,) = local(
            share_kernel, [((rows, width), BF16)], logit_scale, terms, pooled, inverse, smem=(0,)
        )
        return share, slope, columns

    def none(*_):
        return (
            jnp.zeros((rows, width), BF16),
            jnp.zeros((flat, width), BF16),
            jnp.zeros((half, flat), BF16),
        )

    share, slope, columns = lax.cond(
        token_count[0] > 0, own, none, image, alive, norm_gain, head_weight, head_bias
    )
    away_share = lax.ppermute(share, "zh", swap)
    away_slope, away_columns = local(
        partner_kernel,
        [((flat, width), BF16), ((half, flat), BF16)],
        partner,
        norm_gain,
        head_weight,
        head_bias,
    )
    keep, send = local(
        grad_kernel,
        [((half // 2, width), F32), ((half // 2, width), BF16)],
        share,
        slope,
        columns,
        away_share,
        away_slope,
        away_columns,
    )
    away = lax.ppermute(send, "c", swap)
    (parts,) = local(core_kernel, [((size_of("x"), part, width), BF16)], keep, away)
    (grad,) = local(sum_kernel, [((1, part, width), F32)], exchange(parts, "x"))
    return grad


def solution(mesh):
    fine = Mesh(mesh.devices.reshape(SIZES), AXES)
    in_specs = (
        P(AXES, None, None),
        P(AXES),
        P(AXES, None),
        P(),
        P(),
        P(),
        P(),
        P(),
    )
    out_specs = P(("y", "za", "zb"), ("zh", "x", "c"), None)
    return jax.shard_map(
        on_device, mesh=fine, in_specs=in_specs, out_specs=out_specs, check_vma=False
    )
```

```python
import jax
import jax.numpy as jnp
from jax import lax
from jax.experimental import pallas as pl
from jax.experimental.pallas import tpu as pltpu
from jax.sharding import Mesh, PartitionSpec as P

AXES = ("y", "za", "zb", "zh", "x", "c")
SIZES = (4, 4, 4, 2, 4, 2)
VMEM_LIMIT = 60 * 1024 * 1024
COEFF = 0.7978845608
CUBIC = 0.044715
BF16, F32 = jnp.bfloat16, jnp.float32


def size_of(*names):
    count = 1
    for name in names:
        count *= SIZES[AXES.index(name)]
    return count


def from_others(value, axis):
    count = size_of(axis)
    moved = [
        lax.ppermute(value, axis, [(i, (i + k) % count) for i in range(count)])
        for k in range(1, count)
    ]
    return [value] + moved


def exchange(copies, *axes):
    return lax.all_to_all(copies, axes, split_axis=0, concat_axis=0, tiled=True)


def local(body, outs, *args, smem=(), scratch=(), flops=0, moved=0):
    def whole(shape, space):
        return pl.BlockSpec(shape, lambda i: (0,) * len(shape), memory_space=space)

    return pl.pallas_call(
        body,
        grid=(1,),
        out_shape=[jax.ShapeDtypeStruct(shape, dtype) for shape, dtype in outs],
        in_specs=[whole(v.shape, pltpu.SMEM if i in smem else None) for i, v in enumerate(args)],
        out_specs=[whole(shape, None) for shape, _ in outs],
        scratch_shapes=[pltpu.VMEM(shape, dtype) for shape, dtype in scratch],
        compiler_params=pltpu.CompilerParams(vmem_limit_bytes=VMEM_LIMIT),
        cost_estimate=pl.CostEstimate(flops=flops, bytes_accessed=moved, transcendentals=0),
    )(*args)


def image_kernel(image_ref, copies_ref):
    images = image_ref[...].astype(F32)
    norm = jnp.sqrt(jnp.sum(images * images, axis=-1, keepdims=True) + 1e-06)
    image = (images / norm).astype(BF16)
    for k in range(copies_ref.shape[0]):
        copies_ref[k] = image


def front_kernel(
    count_ref, token_ref, gain_ref, weight_ref, bias_ref,
    masked_ref, unit_ref, pooled_ref, inverse_ref, act_ref,
):
    rows, width = pooled_ref.shape
    length = token_ref.shape[0] // rows
    values = token_ref[...].astype(F32)
    center = jnp.mean(values, axis=-1, keepdims=True)
    spread = jnp.mean((values - center) ** 2, axis=-1, keepdims=True)
    gain = gain_ref[...].reshape(1, width)
    normed = ((values - center) * lax.rsqrt(spread + 1e-06) * gain).astype(BF16)
    pre = jnp.dot(normed, weight_ref[...], preferred_element_type=F32)
    pre = pre + bias_ref[...].reshape(1, width)
    act_ref[...] = 0.5 * pre * (1.0 + jnp.tanh(COEFF * (pre + CUBIC * pre * pre * pre)))
    slot = lax.broadcasted_iota(jnp.int32, (length, 1), 0)
    lives = []
    for p in range(rows):
        live = (slot < count_ref[p]).astype(F32)
        inverse = 1.0 / jnp.full((length, 1), count_ref[p], jnp.int32).astype(F32)
        part = act_ref[p * length : (p + 1) * length, :] * (live * inverse)
        pooled_ref[p : p + 1, :] = jnp.sum(part, axis=0, keepdims=True)
        inverse_ref[p : p + 1, :] = jnp.broadcast_to(inverse[:1], (1, inverse_ref.shape[1]))
        lives.append(live)
    masked_ref[...] = normed * jnp.concatenate(lives, axis=0).astype(BF16)
    pooled = pooled_ref[...]
    size = jnp.sqrt(jnp.sum(pooled * pooled, axis=-1, keepdims=True) + 1e-06)
    unit_ref[...] = (pooled / size).astype(BF16)


def slope_kernel(weight_ref, bias_ref, *refs):
    *piece_refs, slope_ref, column_ref = refs
    width = weight_ref.shape[0]
    cores = size_of("c")
    part = column_ref.shape[0] // (2 * cores)
    row = lax.broadcasted_iota(jnp.int32, (2 * cores * part, width), 0)
    source = lax.broadcasted_iota(jnp.int32, (2 * cores * part, width), 1)
    shift = row * 0
    for j in range(cores):
        for far in range(2):
            block = 2 * j + far
            half = (lax.axis_index("zh") + far) % 2
            core = (lax.axis_index("c") + j) % cores
            begin = (half * size_of("x", "c") + lax.axis_index("x") * cores + core) * part
            shift = jnp.where(row >= block * part, begin - block * part, shift)
    pick = jnp.where(source == row + shift, 1.0, 0.0).astype(BF16)
    bias = bias_ref[...].reshape(1, width)
    at = 0
    for ref in piece_refs:
        piece = ref[...]
        block = piece.shape[0]
        pre = jnp.dot(piece, weight_ref[...], preferred_element_type=F32) + bias
        square = pre * pre
        hyper = jnp.tanh(COEFF * (pre + CUBIC * pre * square))
        slope = 0.5 * (1.0 + hyper) + 0.5 * pre * (1.0 - hyper * hyper) * COEFF * (
            1.0 + 3.0 * CUBIC * square
        )
        slope_ref[at : at + block, :] = slope.astype(BF16)
        columns = lax.dot_general(pick, piece, (((1,), (1,)), ((), ())), preferred_element_type=F32)
        column_ref[:, at : at + block] = columns.astype(BF16)
        at += block


def copies_kernel(image_ref, out_ref):
    rows = image_ref.shape[1]
    for k in range(out_ref.shape[0]):
        for j in range(image_ref.shape[0]):
            out_ref[k, j * rows : (j + 1) * rows, :] = image_ref[j]


def logit_kernel(scale_ref, shift_ref, *refs):
    *unit_refs, image_ref, out_ref = refs
    near, rows, width = out_ref.shape
    group = rows * size_of("y", "za", "zb")
    units = jnp.concatenate([ref[...] for ref in unit_refs], axis=0)
    images = image_ref[...]
    temper = jnp.exp(jnp.full((1, 1), scale_ref[0], F32))
    cosine = lax.dot_general(units, images, (((1,), (1,)), ((), ())), preferred_element_type=F32)
    logit = temper * cosine + shift_ref[0]
    unit_at = lax.broadcasted_iota(jnp.int32, cosine.shape, 0)
    image_at = lax.broadcasted_iota(jnp.int32, cosine.shape, 1)
    offset = (lax.axis_index("y") * size_of("za") + lax.axis_index("za")) * rows
    label = jnp.where((unit_at == image_at - offset) & (unit_at < rows), 1.0, -1.0)
    dlogit = (-label / (1.0 + jnp.exp(label * logit)) / group).astype(BF16)
    terms = jnp.dot(dlogit, images, preferred_element_type=F32).astype(BF16)
    for k in range(near):
        owner = lax.rem(lax.axis_index("zb") + near - k, near)
        out_ref[owner] = terms[k * rows : (k + 1) * rows]


def share_kernel(scale_ref, term_ref, pooled_ref, inverse_ref, out_ref):
    temper = jnp.exp(jnp.full((1, 1), scale_ref[0], F32))
    pooled = pooled_ref[...]
    size = jnp.sqrt(jnp.sum(pooled * pooled, axis=-1, keepdims=True) + 1e-06)
    unit = pooled / size
    total = term_ref[0].astype(F32)
    for k in range(1, term_ref.shape[0]):
        total = total + term_ref[k].astype(F32)
    dunit = temper * total
    dpooled = (dunit - unit * jnp.sum(unit * dunit, axis=-1, keepdims=True)) / size
    share = (dpooled * inverse_ref[:, :1]).astype(BF16)
    for k in range(out_ref.shape[0]):
        out_ref[k] = share


def grad_kernel(share_ref, slope_ref, column_ref, keep_ref, send_ref, dpre_ref):
    along, rows, width = share_ref.shape
    block = slope_ref.shape[0] // along
    rest = keep_ref.shape[0]
    for k in range(along):
        owner = lax.rem(lax.axis_index("x") + along - k, along)
        share = share_ref[owner].astype(F32)
        share = jnp.broadcast_to(share[:, None, :], (rows, block // rows, width)).reshape(block, width)
        slope = slope_ref[k * block : (k + 1) * block, :].astype(F32)
        dpre_ref[k * block : (k + 1) * block, :] = (share * slope).astype(BF16)
    total = jnp.dot(column_ref[...], dpre_ref[...], preferred_element_type=F32)
    keep_ref[...] = total[:rest]
    send_ref[...] = total[rest:].astype(BF16)


def core_kernel(keep_ref, away_ref, near_ref, far_ref):
    total = keep_ref[...] + away_ref[...].astype(F32)
    part = near_ref.shape[0]
    near_ref[...] = total[:part]
    far_ref[...] = total[part:].astype(BF16)


def add_kernel(near_ref, away_ref, out_ref):
    out_ref[0] = near_ref[...] + away_ref[...].astype(F32)


def on_device(
    tokens, token_count, image_embed, norm_gain, head_weight, head_bias, logit_scale, logit_bias
):
    rows, length, width = tokens.shape
    part = width // size_of("zh", "x", "c")
    flat = rows * length
    total = size_of("x") * flat
    swap = [(0, 1), (1, 0)]

    (image,) = local(image_kernel, [((size_of("za"), rows, width), BF16)], image_embed)
    tokens, image = lax.optimization_barrier((tokens, image))
    some_images = exchange(image, "za")

    masked, unit, pooled, inverse = local(
        front_kernel,
        [((flat, width), BF16), ((rows, width), BF16), ((rows, width), F32), ((rows, 128), F32)],
        token_count,
        tokens.reshape(flat, width),
        norm_gain,
        head_weight,
        head_bias,
        smem=(0,),
        scratch=[((flat, width), F32)],
        flops=2 * flat * width * width,
        moved=2 * width * width,
    )
    units = from_others(unit, "zb")
    by_x = from_others(masked, "x")
    units, some_images = lax.optimization_barrier((units, some_images))
    (copies,) = local(
        copies_kernel, [((size_of("y"), size_of("za") * rows, width), BF16)], some_images
    )
    all_images = exchange(copies, "y").reshape(-1, width)
    (terms,) = local(
        logit_kernel,
        [((size_of("zb"), rows, width), BF16)],
        logit_scale,
        logit_bias,
        *units,
        all_images,
        smem=(0, 1),
    )
    terms, by_x = lax.optimization_barrier((terms, by_x))
    terms = exchange(terms, "zb")
    slope, columns = local(
        slope_kernel,
        [((total, width), BF16), ((4 * part, total), BF16)],
        head_weight,
        head_bias,
        *by_x,
        flops=2 * total * width * width,
        moved=2 * width * width + 4 * total * width,
    )
    (share,) = local(
        share_kernel,
        [((size_of("x"), rows, width), BF16)],
        logit_scale,
        terms,
        pooled,
        inverse,
        smem=(0,),
    )
    share, slope, columns = lax.optimization_barrier((share, slope, columns))
    shares = exchange(share, "x")
    keep, send = local(
        grad_kernel,
        [((2 * part, width), F32), ((2 * part, width), BF16)],
        shares,
        slope,
        columns,
        scratch=[((total, width), BF16)],
        flops=8 * part * total * width,
        moved=2 * total * width,
    )
    away = lax.ppermute(send, "c", swap)
    near, far = local(core_kernel, [((part, width), F32), ((part, width), BF16)], keep, away)
    away = lax.ppermute(far, "zh", swap)
    (grad,) = local(add_kernel, [((1, part, width), F32)], near, away)
    return grad


def solution(mesh):
    fine = Mesh(mesh.devices.reshape(SIZES), AXES)
    in_specs = (
        P(AXES, None, None),
        P(AXES),
        P(AXES, None),
        P(),
        P(),
        P(),
        P(),
        P(),
    )
    out_specs = P(("y", "za", "zb"), ("zh", "x", "c"), None)
    return jax.shard_map(
        on_device, mesh=fine, in_specs=in_specs, out_specs=out_specs, check_vma=False
    )
```

```python
import jax
import jax.numpy as jnp
from jax import lax
from jax.experimental import pallas as pl
from jax.experimental.pallas import tpu as pltpu
from jax.sharding import Mesh, PartitionSpec as P

AXES = ("y", "za", "zb", "zh", "x", "c")
SIZES = (4, 4, 4, 2, 4, 2)
COEFF = 0.7978845608
CUBIC = 0.044715
BF16, F32 = jnp.bfloat16, jnp.float32


def size_of(*names):
    count = 1
    for name in names:
        count *= SIZES[AXES.index(name)]
    return count


def from_others(value, axis):
    count = size_of(axis)
    moved = [
        lax.ppermute(value, axis, [(i, (i + k) % count) for i in range(count)])
        for k in range(1, count)
    ]
    return [value] + moved


def exchange(copies, *axes):
    return lax.all_to_all(copies, axes, split_axis=0, concat_axis=0, tiled=True)


def local(body, outs, *args, smem=(), scratch=(), flops=0, moved=0, limit=12):
    def whole(shape, space):
        return pl.BlockSpec(shape, lambda i: (0,) * len(shape), memory_space=space)

    return pl.pallas_call(
        body,
        grid=(1,),
        out_shape=[jax.ShapeDtypeStruct(shape, dtype) for shape, dtype in outs],
        in_specs=[whole(v.shape, pltpu.SMEM if i in smem else None) for i, v in enumerate(args)],
        out_specs=[whole(shape, None) for shape, _ in outs],
        scratch_shapes=[pltpu.VMEM(shape, dtype) for shape, dtype in scratch],
        compiler_params=pltpu.CompilerParams(vmem_limit_bytes=limit * 1024 * 1024),
        cost_estimate=pl.CostEstimate(flops=flops, bytes_accessed=moved, transcendentals=0),
    )(*args)


def image_kernel(image_ref, copies_ref):
    images = image_ref[...].astype(F32)
    norm = jnp.sqrt(jnp.sum(images * images, axis=-1, keepdims=True) + 1e-06)
    image = (images / norm).astype(BF16)
    for k in range(copies_ref.shape[0]):
        copies_ref[k] = image


def front_kernel(
    count_ref, token_ref, gain_ref, weight_ref, bias_ref,
    masked_ref, unit_ref, pooled_ref, inverse_ref, act_ref,
):
    rows, width = pooled_ref.shape
    length = token_ref.shape[0] // rows
    values = token_ref[...].astype(F32)
    center = jnp.mean(values, axis=-1, keepdims=True)
    spread = jnp.mean((values - center) ** 2, axis=-1, keepdims=True)
    gain = gain_ref[...].reshape(1, width)
    normed = ((values - center) * lax.rsqrt(spread + 1e-06) * gain).astype(BF16)
    pre = jnp.dot(normed, weight_ref[...], preferred_element_type=F32)
    pre = pre + bias_ref[...].reshape(1, width)
    act_ref[...] = 0.5 * pre * (1.0 + jnp.tanh(COEFF * (pre + CUBIC * pre * pre * pre)))
    slot = lax.broadcasted_iota(jnp.int32, (length, 1), 0)
    lives = []
    for p in range(rows):
        live = (slot < count_ref[p]).astype(F32)
        inverse = 1.0 / jnp.full((length, 1), count_ref[p], jnp.int32).astype(F32)
        part = act_ref[p * length : (p + 1) * length, :] * (live * inverse)
        pooled_ref[p : p + 1, :] = jnp.sum(part, axis=0, keepdims=True)
        inverse_ref[p : p + 1, :] = jnp.broadcast_to(inverse[:1], (1, inverse_ref.shape[1]))
        lives.append(live)
    masked_ref[...] = normed * jnp.concatenate(lives, axis=0).astype(BF16)
    pooled = pooled_ref[...]
    size = jnp.sqrt(jnp.sum(pooled * pooled, axis=-1, keepdims=True) + 1e-06)
    unit_ref[...] = (pooled / size).astype(BF16)


def slope_kernel(weight_ref, bias_ref, *refs):
    *piece_refs, slope_ref, column_ref = refs
    width = weight_ref.shape[0]
    cores = size_of("c")
    part = column_ref.shape[0] // (2 * cores)
    row = lax.broadcasted_iota(jnp.int32, (2 * cores * part, width), 0)
    source = lax.broadcasted_iota(jnp.int32, (2 * cores * part, width), 1)
    shift = row * 0
    for j in range(cores):
        for far in range(2):
            block = 2 * j + far
            half = (lax.axis_index("zh") + far) % 2
            core = (lax.axis_index("c") + j) % cores
            begin = (half * size_of("x", "c") + lax.axis_index("x") * cores + core) * part
            shift = jnp.where(row >= block * part, begin - block * part, shift)
    pick = jnp.where(source == row + shift, 1.0, 0.0).astype(BF16)
    bias = bias_ref[...].reshape(1, width)
    at = 0
    for ref in piece_refs:
        piece = ref[...]
        block = piece.shape[0]
        pre = jnp.dot(piece, weight_ref[...], preferred_element_type=F32) + bias
        square = pre * pre
        hyper = jnp.tanh(COEFF * (pre + CUBIC * pre * square))
        slope = 0.5 * (1.0 + hyper) + 0.5 * pre * (1.0 - hyper * hyper) * COEFF * (
            1.0 + 3.0 * CUBIC * square
        )
        slope_ref[at : at + block, :] = slope.astype(BF16)
        columns = lax.dot_general(pick, piece, (((1,), (1,)), ((), ())), preferred_element_type=F32)
        column_ref[:, at : at + block] = columns.astype(BF16)
        at += block


def copies_kernel(image_ref, out_ref):
    rows = image_ref.shape[1]
    for k in range(out_ref.shape[0]):
        for j in range(image_ref.shape[0]):
            out_ref[k, j * rows : (j + 1) * rows, :] = image_ref[j]


def logit_kernel(scale_ref, shift_ref, *refs):
    *unit_refs, image_ref, out_ref = refs
    near, rows, width = out_ref.shape
    group = rows * size_of("y", "za", "zb")
    units = jnp.concatenate([ref[...] for ref in unit_refs], axis=0)
    images = image_ref[...]
    temper = jnp.exp(jnp.full((1, 1), scale_ref[0], F32))
    cosine = lax.dot_general(units, images, (((1,), (1,)), ((), ())), preferred_element_type=F32)
    logit = temper * cosine + shift_ref[0]
    unit_at = lax.broadcasted_iota(jnp.int32, cosine.shape, 0)
    image_at = lax.broadcasted_iota(jnp.int32, cosine.shape, 1)
    offset = (lax.axis_index("y") * size_of("za") + lax.axis_index("za")) * rows
    label = jnp.where((unit_at == image_at - offset) & (unit_at < rows), 1.0, -1.0)
    dlogit = (-label / (1.0 + jnp.exp(label * logit)) / group).astype(BF16)
    terms = jnp.dot(dlogit, images, preferred_element_type=F32).astype(BF16)
    for k in range(near):
        owner = lax.rem(lax.axis_index("zb") + near - k, near)
        out_ref[owner] = terms[k * rows : (k + 1) * rows]


def share_kernel(scale_ref, term_ref, pooled_ref, inverse_ref, out_ref):
    temper = jnp.exp(jnp.full((1, 1), scale_ref[0], F32))
    pooled = pooled_ref[...]
    size = jnp.sqrt(jnp.sum(pooled * pooled, axis=-1, keepdims=True) + 1e-06)
    unit = pooled / size
    total = term_ref[0].astype(F32)
    for k in range(1, term_ref.shape[0]):
        total = total + term_ref[k].astype(F32)
    dunit = temper * total
    dpooled = (dunit - unit * jnp.sum(unit * dunit, axis=-1, keepdims=True)) / size
    share = (dpooled * inverse_ref[:, :1]).astype(BF16)
    for k in range(out_ref.shape[0]):
        out_ref[k] = share


def grad_kernel(share_ref, slope_ref, column_ref, keep_ref, send_ref, dpre_ref):
    along, rows, width = share_ref.shape
    block = slope_ref.shape[0] // along
    rest = keep_ref.shape[0]
    for k in range(along):
        owner = lax.rem(lax.axis_index("x") + along - k, along)
        share = share_ref[owner].astype(F32)
        share = jnp.broadcast_to(share[:, None, :], (rows, block // rows, width)).reshape(block, width)
        slope = slope_ref[k * block : (k + 1) * block, :].astype(F32)
        dpre_ref[k * block : (k + 1) * block, :] = (share * slope).astype(BF16)
    total = jnp.dot(column_ref[...], dpre_ref[...], preferred_element_type=F32)
    keep_ref[...] = total[:rest]
    send_ref[...] = total[rest:].astype(BF16)


def core_kernel(keep_ref, away_ref, near_ref, far_ref):
    total = keep_ref[...] + away_ref[...].astype(F32)
    part = near_ref.shape[0]
    near_ref[...] = total[:part]
    far_ref[...] = total[part:].astype(BF16)


def add_kernel(near_ref, away_ref, out_ref):
    out_ref[0] = near_ref[...] + away_ref[...].astype(F32)


def on_device(
    tokens, token_count, image_embed, norm_gain, head_weight, head_bias, logit_scale, logit_bias
):
    rows, length, width = tokens.shape
    part = width // size_of("zh", "x", "c")
    flat = rows * length
    total = size_of("x") * flat
    swap = [(0, 1), (1, 0)]

    (image,) = local(image_kernel, [((size_of("za"), rows, width), BF16)], image_embed)
    tokens, image = lax.optimization_barrier((tokens, image))
    some_images = exchange(image, "za")

    masked, unit, pooled, inverse = local(
        front_kernel,
        [((flat, width), BF16), ((rows, width), BF16), ((rows, width), F32), ((rows, 128), F32)],
        token_count,
        tokens.reshape(flat, width),
        norm_gain,
        head_weight,
        head_bias,
        smem=(0,),
        scratch=[((flat, width), F32)],
        flops=2 * flat * width * width,
        moved=2 * width * width,
        limit=60,
    )
    units = from_others(unit, "zb")
    by_x = from_others(masked, "x")
    mine, *early, last = by_x
    early, units, some_images = lax.optimization_barrier((early, units, some_images))
    by_x = [mine, *early, last]
    (copies,) = local(
        copies_kernel, [((size_of("y"), size_of("za") * rows, width), BF16)], some_images
    )
    all_images = exchange(copies, "y").reshape(-1, width)
    (terms,) = local(
        logit_kernel,
        [((size_of("zb"), rows, width), BF16)],
        logit_scale,
        logit_bias,
        *units,
        all_images,
        smem=(0, 1),
    )
    terms, by_x = lax.optimization_barrier((terms, by_x))
    terms = exchange(terms, "zb")
    slope, columns = local(
        slope_kernel,
        [((total, width), BF16), ((4 * part, total), BF16)],
        head_weight,
        head_bias,
        *by_x,
        flops=2 * total * width * width,
        moved=2 * width * width + 4 * total * width,
        limit=60,
    )
    (share,) = local(
        share_kernel,
        [((size_of("x"), rows, width), BF16)],
        logit_scale,
        terms,
        pooled,
        inverse,
        smem=(0,),
    )
    share, slope, columns = lax.optimization_barrier((share, slope, columns))
    shares = exchange(share, "x")
    keep, send = local(
        grad_kernel,
        [((2 * part, width), F32), ((2 * part, width), BF16)],
        shares,
        slope,
        columns,
        scratch=[((total, width), BF16)],
        flops=8 * part * total * width,
        moved=2 * total * width,
        limit=24,
    )
    away = lax.ppermute(send, "c", swap)
    near, far = local(core_kernel, [((part, width), F32), ((part, width), BF16)], keep, away)
    away = lax.ppermute(far, "zh", swap)
    (grad,) = local(add_kernel, [((1, part, width), F32)], near, away)
    return grad


def solution(mesh):
    fine = Mesh(mesh.devices.reshape(SIZES), AXES)
    in_specs = (
        P(AXES, None, None),
        P(AXES),
        P(AXES, None),
        P(),
        P(),
        P(),
        P(),
        P(),
    )
    out_specs = P(("y", "za", "zb"), ("zh", "x", "c"), None)
    return jax.shard_map(
        on_device, mesh=fine, in_specs=in_specs, out_specs=out_specs, check_vma=False
    )
```

```python
import jax
import jax.numpy as jnp
from jax import lax
from jax.experimental import pallas as pl
from jax.experimental.pallas import tpu as pltpu
from jax.sharding import Mesh, PartitionSpec as P

AXES = ("y", "za", "zb", "zh", "x", "c")
SIZES = (4, 4, 4, 2, 4, 2)
COEFF = 0.7978845608
CUBIC = 0.044715
BF16, F32 = jnp.bfloat16, jnp.float32


def size_of(*names):
    count = 1
    for name in names:
        count *= SIZES[AXES.index(name)]
    return count


def from_others(value, axis):
    count = size_of(axis)
    moved = [
        lax.ppermute(value, axis, [(i, (i + k) % count) for i in range(count)])
        for k in range(1, count)
    ]
    return [value] + moved


def exchange(copies, *axes):
    return lax.all_to_all(copies, axes, split_axis=0, concat_axis=0, tiled=True)


def local(body, outs, *args, smem=(), scratch=(), flops=0, moved=0, limit=12):
    def whole(shape, space):
        return pl.BlockSpec(shape, lambda i: (0,) * len(shape), memory_space=space)

    return pl.pallas_call(
        body,
        grid=(1,),
        out_shape=[jax.ShapeDtypeStruct(shape, dtype) for shape, dtype in outs],
        in_specs=[whole(v.shape, pltpu.SMEM if i in smem else None) for i, v in enumerate(args)],
        out_specs=[whole(shape, None) for shape, _ in outs],
        scratch_shapes=[pltpu.VMEM(shape, dtype) for shape, dtype in scratch],
        compiler_params=pltpu.CompilerParams(vmem_limit_bytes=limit * 1024 * 1024),
        cost_estimate=pl.CostEstimate(flops=flops, bytes_accessed=moved, transcendentals=0),
    )(*args)


def image_kernel(image_ref, copies_ref):
    images = image_ref[...].astype(F32)
    norm = jnp.sqrt(jnp.sum(images * images, axis=-1, keepdims=True) + 1e-06)
    image = (images / norm).astype(BF16)
    for k in range(copies_ref.shape[0]):
        copies_ref[k] = image


def front_kernel(
    count_ref, token_ref, gain_ref, weight_ref, bias_ref,
    masked_ref, unit_ref, pooled_ref, inverse_ref, act_ref,
):
    rows, width = pooled_ref.shape
    length = token_ref.shape[0] // rows
    values = token_ref[...].astype(F32)
    center = jnp.mean(values, axis=-1, keepdims=True)
    spread = jnp.mean((values - center) ** 2, axis=-1, keepdims=True)
    gain = gain_ref[...].reshape(1, width)
    normed = ((values - center) * lax.rsqrt(spread + 1e-06) * gain).astype(BF16)
    pre = jnp.dot(normed, weight_ref[...], preferred_element_type=F32)
    pre = pre + bias_ref[...].reshape(1, width)
    act_ref[...] = 0.5 * pre * (1.0 + jnp.tanh(COEFF * (pre + CUBIC * pre * pre * pre)))
    slot = lax.broadcasted_iota(jnp.int32, (length, 1), 0)
    lives = []
    for p in range(rows):
        live = (slot < count_ref[p]).astype(F32)
        inverse = 1.0 / jnp.full((length, 1), count_ref[p], jnp.int32).astype(F32)
        part = act_ref[p * length : (p + 1) * length, :] * (live * inverse)
        pooled_ref[p : p + 1, :] = jnp.sum(part, axis=0, keepdims=True)
        inverse_ref[p : p + 1, :] = jnp.broadcast_to(inverse[:1], (1, inverse_ref.shape[1]))
        lives.append(live)
    masked_ref[...] = normed * jnp.concatenate(lives, axis=0).astype(BF16)
    pooled = pooled_ref[...]
    size = jnp.sqrt(jnp.sum(pooled * pooled, axis=-1, keepdims=True) + 1e-06)
    unit_ref[...] = (pooled / size).astype(BF16)


def slope_kernel(weight_ref, bias_ref, *refs):
    *piece_refs, slope_ref, column_ref = refs
    width = weight_ref.shape[0]
    cores = size_of("c")
    part = column_ref.shape[0] // (2 * cores)
    row = lax.broadcasted_iota(jnp.int32, (2 * cores * part, width), 0)
    source = lax.broadcasted_iota(jnp.int32, (2 * cores * part, width), 1)
    shift = row * 0
    for j in range(cores):
        for far in range(2):
            block = 2 * j + far
            half = (lax.axis_index("zh") + far) % 2
            core = (lax.axis_index("c") + j) % cores
            begin = (half * size_of("x", "c") + lax.axis_index("x") * cores + core) * part
            shift = jnp.where(row >= block * part, begin - block * part, shift)
    pick = jnp.where(source == row + shift, 1.0, 0.0).astype(BF16)
    bias = bias_ref[...].reshape(1, width)
    at = 0
    for ref in piece_refs:
        piece = ref[...]
        block = piece.shape[0]
        pre = jnp.dot(piece, weight_ref[...], preferred_element_type=F32) + bias
        square = pre * pre
        hyper = jnp.tanh(COEFF * (pre + CUBIC * pre * square))
        slope = 0.5 * (1.0 + hyper) + 0.5 * pre * (1.0 - hyper * hyper) * COEFF * (
            1.0 + 3.0 * CUBIC * square
        )
        slope_ref[at : at + block, :] = slope.astype(BF16)
        columns = lax.dot_general(pick, piece, (((1,), (1,)), ((), ())), preferred_element_type=F32)
        column_ref[:, at : at + block] = columns.astype(BF16)
        at += block


def copies_kernel(image_ref, out_ref):
    rows = image_ref.shape[1]
    for k in range(out_ref.shape[0]):
        for j in range(image_ref.shape[0]):
            out_ref[k, j * rows : (j + 1) * rows, :] = image_ref[j]


def logit_kernel(scale_ref, shift_ref, *refs):
    *unit_refs, image_ref, out_ref = refs
    near, rows, width = out_ref.shape
    group = rows * size_of("y", "za", "zb")
    units = jnp.concatenate([ref[...] for ref in unit_refs], axis=0)
    images = image_ref[...]
    temper = jnp.exp(jnp.full((1, 1), scale_ref[0], F32))
    cosine = lax.dot_general(units, images, (((1,), (1,)), ((), ())), preferred_element_type=F32)
    logit = temper * cosine + shift_ref[0]
    unit_at = lax.broadcasted_iota(jnp.int32, cosine.shape, 0)
    image_at = lax.broadcasted_iota(jnp.int32, cosine.shape, 1)
    offset = (lax.axis_index("y") * size_of("za") + lax.axis_index("za")) * rows
    label = jnp.where((unit_at == image_at - offset) & (unit_at < rows), 1.0, -1.0)
    dlogit = (-label / (1.0 + jnp.exp(label * logit)) / group).astype(BF16)
    terms = jnp.dot(dlogit, images, preferred_element_type=F32).astype(BF16)
    for k in range(near):
        owner = lax.rem(lax.axis_index("zb") + near - k, near)
        out_ref[owner] = terms[k * rows : (k + 1) * rows]


def share_kernel(scale_ref, term_ref, pooled_ref, inverse_ref, out_ref):
    temper = jnp.exp(jnp.full((1, 1), scale_ref[0], F32))
    pooled = pooled_ref[...]
    size = jnp.sqrt(jnp.sum(pooled * pooled, axis=-1, keepdims=True) + 1e-06)
    unit = pooled / size
    total = term_ref[0].astype(F32)
    for k in range(1, term_ref.shape[0]):
        total = total + term_ref[k].astype(F32)
    dunit = temper * total
    dpooled = (dunit - unit * jnp.sum(unit * dunit, axis=-1, keepdims=True)) / size
    share = (dpooled * inverse_ref[:, :1]).astype(BF16)
    for k in range(out_ref.shape[0]):
        out_ref[k] = share


def grad_kernel(share_ref, slope_ref, column_ref, keep_ref, send_ref, dpre_ref):
    along, rows, width = share_ref.shape
    block = slope_ref.shape[0] // along
    rest = keep_ref.shape[0]
    for k in range(along):
        owner = lax.rem(lax.axis_index("x") + along - k, along)
        share = share_ref[owner].astype(F32)
        share = jnp.broadcast_to(share[:, None, :], (rows, block // rows, width)).reshape(block, width)
        slope = slope_ref[k * block : (k + 1) * block, :].astype(F32)
        dpre_ref[k * block : (k + 1) * block, :] = (share * slope).astype(BF16)
    total = jnp.dot(column_ref[...], dpre_ref[...], preferred_element_type=F32)
    keep_ref[...] = total[:rest]
    send_ref[...] = total[rest:].astype(BF16)


def core_kernel(keep_ref, away_ref, near_ref, far_ref):
    total = keep_ref[...] + away_ref[...].astype(F32)
    part = near_ref.shape[0]
    near_ref[...] = total[:part]
    far_ref[...] = total[part:].astype(BF16)


def add_kernel(near_ref, away_ref, out_ref):
    out_ref[0] = near_ref[...] + away_ref[...].astype(F32)


def on_device(
    tokens, token_count, image_embed, norm_gain, head_weight, head_bias, logit_scale, logit_bias
):
    rows, length, width = tokens.shape
    part = width // size_of("zh", "x", "c")
    flat = rows * length
    total = size_of("x") * flat
    swap = [(0, 1), (1, 0)]

    (image,) = local(image_kernel, [((size_of("za"), rows, width), BF16)], image_embed)
    tokens, image = lax.optimization_barrier((tokens, image))
    some_images = exchange(image, "za")

    masked, unit, pooled, inverse = local(
        front_kernel,
        [((flat, width), BF16), ((rows, width), BF16), ((rows, width), F32), ((rows, 128), F32)],
        token_count,
        tokens.reshape(flat, width),
        norm_gain,
        head_weight,
        head_bias,
        smem=(0,),
        scratch=[((flat, width), F32)],
        flops=2 * flat * width * width,
        moved=2 * width * width,
        limit=60,
    )
    units = from_others(unit, "zb")
    by_x = from_others(masked, "x")
    units, some_images = lax.optimization_barrier((units, some_images))
    (copies,) = local(
        copies_kernel, [((size_of("y"), size_of("za") * rows, width), BF16)], some_images
    )
    all_images = exchange(copies, "y").reshape(-1, width)
    (terms,) = local(
        logit_kernel,
        [((size_of("zb"), rows, width), BF16)],
        logit_scale,
        logit_bias,
        *units,
        all_images,
        smem=(0, 1),
    )
    mine, first, *rest = by_x
    terms, rest = lax.optimization_barrier((terms, rest))
    by_x = [mine, first, *rest]
    terms = exchange(terms, "zb")
    slope, columns = local(
        slope_kernel,
        [((total, width), BF16), ((4 * part, total), BF16)],
        head_weight,
        head_bias,
        *by_x,
        flops=2 * total * width * width,
        moved=2 * width * width + 4 * total * width,
        limit=60,
    )
    (share,) = local(
        share_kernel,
        [((size_of("x"), rows, width), BF16)],
        logit_scale,
        terms,
        pooled,
        inverse,
        smem=(0,),
    )
    shares = exchange(share, "x")
    keep, send = local(
        grad_kernel,
        [((2 * part, width), F32), ((2 * part, width), BF16)],
        shares,
        slope,
        columns,
        scratch=[((total, width), BF16)],
        flops=8 * part * total * width,
        moved=2 * total * width,
        limit=24,
    )
    away = lax.ppermute(send, "c", swap)
    near, far = local(core_kernel, [((part, width), F32), ((part, width), BF16)], keep, away)
    away = lax.ppermute(far, "zh", swap)
    (grad,) = local(add_kernel, [((1, part, width), F32)], near, away)
    return grad


def solution(mesh):
    fine = Mesh(mesh.devices.reshape(SIZES), AXES)
    in_specs = (
        P(AXES, None, None),
        P(AXES),
        P(AXES, None),
        P(),
        P(),
        P(),
        P(),
        P(),
    )
    out_specs = P(("y", "za", "zb"), ("zh", "x", "c"), None)
    return jax.shard_map(
        on_device, mesh=fine, in_specs=in_specs, out_specs=out_specs, check_vma=False
    )
```

```python
import jax
import jax.numpy as jnp
from jax import lax
from jax.experimental import pallas as pl
from jax.experimental.pallas import tpu as pltpu
from jax.sharding import Mesh, PartitionSpec as P

AXES = ("y", "za", "zb", "zh", "x", "c")
SIZES = (4, 4, 4, 2, 4, 2)
COEFF = 0.7978845608
CUBIC = 0.044715
BF16, F32 = jnp.bfloat16, jnp.float32


def size_of(*names):
    count = 1
    for name in names:
        count *= SIZES[AXES.index(name)]
    return count


def from_others(value, axis):
    count = size_of(axis)
    moved = [
        lax.ppermute(value, axis, [(i, (i + k) % count) for i in range(count)])
        for k in range(1, count)
    ]
    return [value] + moved


def exchange(copies, *axes):
    return lax.all_to_all(copies, axes, split_axis=0, concat_axis=0, tiled=True)


def local(body, outs, *args, smem=(), scratch=(), flops=0, moved=0, limit=12):
    def whole(shape, space):
        return pl.BlockSpec(shape, lambda i: (0,) * len(shape), memory_space=space)

    return pl.pallas_call(
        body,
        grid=(1,),
        out_shape=[jax.ShapeDtypeStruct(shape, dtype) for shape, dtype in outs],
        in_specs=[whole(v.shape, pltpu.SMEM if i in smem else None) for i, v in enumerate(args)],
        out_specs=[whole(shape, None) for shape, _ in outs],
        scratch_shapes=[pltpu.VMEM(shape, dtype) for shape, dtype in scratch],
        compiler_params=pltpu.CompilerParams(vmem_limit_bytes=limit * 1024 * 1024),
        cost_estimate=pl.CostEstimate(flops=flops, bytes_accessed=moved, transcendentals=0),
    )(*args)


def image_kernel(image_ref, copies_ref):
    images = image_ref[...].astype(F32)
    norm = jnp.sqrt(jnp.sum(images * images, axis=-1, keepdims=True) + 1e-06)
    image = (images / norm).astype(BF16)
    for k in range(copies_ref.shape[0]):
        copies_ref[k] = image


def front_kernel(
    count_ref, scale_ref, shift_ref, token_ref, gain_ref, weight_ref, bias_ref,
    masked_ref, unit_ref, pooled_ref, inverse_ref, act_ref,
):
    rows, width = pooled_ref.shape
    length = token_ref.shape[0] // rows
    values = token_ref[...].astype(F32)
    center = jnp.mean(values, axis=-1, keepdims=True)
    spread = jnp.mean((values - center) ** 2, axis=-1, keepdims=True)
    gain = gain_ref[...].reshape(1, width)
    normed = ((values - center) * lax.rsqrt(spread + 1e-06) * gain).astype(BF16)
    pre = jnp.dot(normed, weight_ref[...], preferred_element_type=F32)
    pre = pre + bias_ref[...].reshape(1, width)
    act_ref[...] = 0.5 * pre * (1.0 + jnp.tanh(COEFF * (pre + CUBIC * pre * pre * pre)))
    lane = lax.broadcasted_iota(jnp.int32, (1, inverse_ref.shape[1]), 1)
    temper = jnp.exp(jnp.full(lane.shape, scale_ref[0], F32))
    scalars = jnp.where(lane == 1, temper, shift_ref[0])
    slot = lax.broadcasted_iota(jnp.int32, (length, 1), 0)
    lives = []
    for p in range(rows):
        live = (slot < count_ref[p]).astype(F32)
        inverse = 1.0 / jnp.full((length, 1), count_ref[p], jnp.int32).astype(F32)
        part = act_ref[p * length : (p + 1) * length, :] * (live * inverse)
        pooled_ref[p : p + 1, :] = jnp.sum(part, axis=0, keepdims=True)
        inverse_ref[p : p + 1, :] = jnp.where(lane == 0, inverse[:1], scalars)
        lives.append(live)
    masked_ref[...] = normed * jnp.concatenate(lives, axis=0).astype(BF16)
    pooled = pooled_ref[...]
    size = jnp.sqrt(jnp.sum(pooled * pooled, axis=-1, keepdims=True) + 1e-06)
    unit_ref[...] = (pooled / size).astype(BF16)


def slope_kernel(weight_ref, bias_ref, *refs):
    *piece_refs, slope_ref, column_ref = refs
    width = weight_ref.shape[0]
    cores = size_of("c")
    part = column_ref.shape[0] // (2 * cores)
    row = lax.broadcasted_iota(jnp.int32, (2 * cores * part, width), 0)
    source = lax.broadcasted_iota(jnp.int32, (2 * cores * part, width), 1)
    shift = row * 0
    for j in range(cores):
        for far in range(2):
            block = 2 * j + far
            half = (lax.axis_index("zh") + far) % 2
            core = (lax.axis_index("c") + j) % cores
            begin = (half * size_of("x", "c") + lax.axis_index("x") * cores + core) * part
            shift = jnp.where(row >= block * part, begin - block * part, shift)
    pick = jnp.where(source == row + shift, 1.0, 0.0).astype(BF16)
    bias = bias_ref[...].reshape(1, width)
    at = 0
    for ref in piece_refs:
        piece = ref[...]
        block = piece.shape[0]
        pre = jnp.dot(piece, weight_ref[...], preferred_element_type=F32) + bias
        square = pre * pre
        hyper = jnp.tanh(COEFF * (pre + CUBIC * pre * square))
        slope = 0.5 * (1.0 + hyper) + 0.5 * pre * (1.0 - hyper * hyper) * COEFF * (
            1.0 + 3.0 * CUBIC * square
        )
        slope_ref[at : at + block, :] = slope.astype(BF16)
        columns = lax.dot_general(pick, piece, (((1,), (1,)), ((), ())), preferred_element_type=F32)
        column_ref[:, at : at + block] = columns.astype(BF16)
        at += block


def copies_kernel(image_ref, out_ref):
    rows = image_ref.shape[1]
    for k in range(out_ref.shape[0]):
        for j in range(image_ref.shape[0]):
            out_ref[k, j * rows : (j + 1) * rows, :] = image_ref[j]


def logit_kernel(scalar_ref, *refs):
    *unit_refs, image_ref, out_ref = refs
    near, rows, width = out_ref.shape
    group = rows * size_of("y", "za", "zb")
    units = jnp.concatenate([ref[...] for ref in unit_refs], axis=0)
    images = image_ref[...]
    cosine = lax.dot_general(units, images, (((1,), (1,)), ((), ())), preferred_element_type=F32)
    logit = scalar_ref[:1, 1:2] * cosine + scalar_ref[:1, 2:3]
    unit_at = lax.broadcasted_iota(jnp.int32, cosine.shape, 0)
    image_at = lax.broadcasted_iota(jnp.int32, cosine.shape, 1)
    offset = (lax.axis_index("y") * size_of("za") + lax.axis_index("za")) * rows
    label = jnp.where((unit_at == image_at - offset) & (unit_at < rows), 1.0, -1.0)
    dlogit = (-label / (1.0 + jnp.exp(label * logit)) / group).astype(BF16)
    terms = jnp.dot(dlogit, images, preferred_element_type=F32).astype(BF16)
    for k in range(near):
        owner = lax.rem(lax.axis_index("zb") + near - k, near)
        out_ref[owner] = terms[k * rows : (k + 1) * rows]


def share_kernel(term_ref, pooled_ref, inverse_ref, out_ref):
    pooled = pooled_ref[...]
    size = jnp.sqrt(jnp.sum(pooled * pooled, axis=-1, keepdims=True) + 1e-06)
    unit = pooled / size
    total = term_ref[0].astype(F32)
    for k in range(1, term_ref.shape[0]):
        total = total + term_ref[k].astype(F32)
    dunit = inverse_ref[:, 1:2] * total
    dpooled = (dunit - unit * jnp.sum(unit * dunit, axis=-1, keepdims=True)) / size
    share = (dpooled * inverse_ref[:, :1]).astype(BF16)
    for k in range(out_ref.shape[0]):
        out_ref[k] = share


def grad_kernel(share_ref, slope_ref, column_ref, keep_ref, send_ref, dpre_ref):
    along, rows, width = share_ref.shape
    block = slope_ref.shape[0] // along
    rest = keep_ref.shape[0]
    for k in range(along):
        owner = lax.rem(lax.axis_index("x") + along - k, along)
        share = share_ref[owner].astype(F32)
        share = jnp.broadcast_to(share[:, None, :], (rows, block // rows, width)).reshape(block, width)
        slope = slope_ref[k * block : (k + 1) * block, :].astype(F32)
        dpre_ref[k * block : (k + 1) * block, :] = (share * slope).astype(BF16)
    total = jnp.dot(column_ref[...], dpre_ref[...], preferred_element_type=F32)
    keep_ref[...] = total[:rest]
    send_ref[...] = total[rest:].astype(BF16)


def core_kernel(keep_ref, away_ref, near_ref, far_ref):
    total = keep_ref[...] + away_ref[...].astype(F32)
    part = near_ref.shape[0]
    near_ref[...] = total[:part]
    far_ref[...] = total[part:].astype(BF16)


def add_kernel(near_ref, away_ref, out_ref):
    out_ref[0] = near_ref[...] + away_ref[...].astype(F32)


def on_device(
    tokens, token_count, image_embed, norm_gain, head_weight, head_bias, logit_scale, logit_bias
):
    rows, length, width = tokens.shape
    part = width // size_of("zh", "x", "c")
    flat = rows * length
    total = size_of("x") * flat
    swap = [(0, 1), (1, 0)]

    (image,) = local(image_kernel, [((size_of("za"), rows, width), BF16)], image_embed)
    tokens, image = lax.optimization_barrier((tokens, image))
    some_images = exchange(image, "za")

    masked, unit, pooled, inverse = local(
        front_kernel,
        [((flat, width), BF16), ((rows, width), BF16), ((rows, width), F32), ((rows, 128), F32)],
        token_count,
        logit_scale,
        logit_bias,
        tokens.reshape(flat, width),
        norm_gain,
        head_weight,
        head_bias,
        smem=(0, 1, 2),
        scratch=[((flat, width), F32)],
        flops=2 * flat * width * width,
        moved=2 * width * width,
        limit=60,
    )
    units = from_others(unit, "zb")
    by_x = from_others(masked, "x")
    units, some_images = lax.optimization_barrier((units, some_images))
    (copies,) = local(
        copies_kernel, [((size_of("y"), size_of("za") * rows, width), BF16)], some_images
    )
    all_images = exchange(copies, "y").reshape(-1, width)
    (terms,) = local(
        logit_kernel,
        [((size_of("zb"), rows, width), BF16)],
        inverse,
        *units,
        all_images,
    )
    terms, by_x[-1] = lax.optimization_barrier((terms, by_x[-1]))
    terms = exchange(terms, "zb")
    slope, columns = local(
        slope_kernel,
        [((total, width), BF16), ((4 * part, total), BF16)],
        head_weight,
        head_bias,
        *by_x,
        flops=2 * total * width * width,
        moved=2 * width * width + 4 * total * width,
        limit=60,
    )
    (share,) = local(
        share_kernel,
        [((size_of("x"), rows, width), BF16)],
        terms,
        pooled,
        inverse,
    )
    shares = exchange(share, "x")
    keep, send = local(
        grad_kernel,
        [((2 * part, width), F32), ((2 * part, width), BF16)],
        shares,
        slope,
        columns,
        scratch=[((total, width), BF16)],
        flops=8 * part * total * width,
        moved=2 * total * width,
        limit=24,
    )
    away = lax.ppermute(send, "c", swap)
    near, far = local(core_kernel, [((part, width), F32), ((part, width), BF16)], keep, away)
    away = lax.ppermute(far, "zh", swap)
    (grad,) = local(add_kernel, [((1, part, width), F32)], near, away)
    return grad


def solution(mesh):
    fine = Mesh(mesh.devices.reshape(SIZES), AXES)
    in_specs = (
        P(AXES, None, None),
        P(AXES),
        P(AXES, None),
        P(),
        P(),
        P(),
        P(),
        P(),
    )
    out_specs = P(("y", "za", "zb"), ("zh", "x", "c"), None)
    return jax.shard_map(
        on_device, mesh=fine, in_specs=in_specs, out_specs=out_specs, check_vma=False
    )
```

```python
import jax
import jax.numpy as jnp
from jax import lax
from jax.experimental import pallas as pl
from jax.experimental.pallas import tpu as pltpu
from jax.sharding import Mesh, PartitionSpec as P

AXES = ("y", "za", "zb", "zh", "x", "c")
SIZES = (4, 4, 4, 2, 4, 2)
COEFF = 0.7978845608
CUBIC = 0.044715
BF16, F32 = jnp.bfloat16, jnp.float32


def size_of(*names):
    count = 1
    for name in names:
        count *= SIZES[AXES.index(name)]
    return count


def from_others(value, axis):
    count = size_of(axis)
    moved = [
        lax.ppermute(value, axis, [(i, (i + k) % count) for i in range(count)])
        for k in range(1, count)
    ]
    return [value] + moved


def exchange(copies, *axes):
    return lax.all_to_all(copies, axes, split_axis=0, concat_axis=0, tiled=True)


def local(body, outs, *args, smem=(), scratch=(), flops=0, moved=0, limit=12):
    def whole(shape, space):
        return pl.BlockSpec(shape, lambda i: (0,) * len(shape), memory_space=space)

    return pl.pallas_call(
        body,
        grid=(1,),
        out_shape=[jax.ShapeDtypeStruct(shape, dtype) for shape, dtype in outs],
        in_specs=[whole(v.shape, pltpu.SMEM if i in smem else None) for i, v in enumerate(args)],
        out_specs=[whole(shape, None) for shape, _ in outs],
        scratch_shapes=[pltpu.VMEM(shape, dtype) for shape, dtype in scratch],
        compiler_params=pltpu.CompilerParams(vmem_limit_bytes=limit * 1024 * 1024),
        cost_estimate=pl.CostEstimate(flops=flops, bytes_accessed=moved, transcendentals=0),
    )(*args)


def image_kernel(image_ref, copies_ref):
    images = image_ref[...].astype(F32)
    norm = jnp.sqrt(jnp.sum(images * images, axis=-1, keepdims=True) + 1e-06)
    image = (images / norm).astype(BF16)
    for k in range(copies_ref.shape[0]):
        copies_ref[k] = image


def front_kernel(
    count_ref, token_ref, gain_ref, weight_ref, bias_ref,
    masked_ref, unit_ref, pooled_ref, inverse_ref, act_ref,
):
    rows, width = pooled_ref.shape
    length = token_ref.shape[0] // rows
    values = token_ref[...].astype(F32)
    center = jnp.mean(values, axis=-1, keepdims=True)
    spread = jnp.mean((values - center) ** 2, axis=-1, keepdims=True)
    gain = gain_ref[...].reshape(1, width)
    normed = ((values - center) * lax.rsqrt(spread + 1e-06) * gain).astype(BF16)
    pre = jnp.dot(normed, weight_ref[...], preferred_element_type=F32)
    pre = pre + bias_ref[...].reshape(1, width)
    act_ref[...] = 0.5 * pre * (1.0 + jnp.tanh(COEFF * (pre + CUBIC * pre * pre * pre)))
    slot = lax.broadcasted_iota(jnp.int32, (length, 1), 0)
    lives = []
    for p in range(rows):
        live = (slot < count_ref[p]).astype(F32)
        inverse = 1.0 / jnp.full((length, 1), count_ref[p], jnp.int32).astype(F32)
        part = act_ref[p * length : (p + 1) * length, :] * (live * inverse)
        pooled_ref[p : p + 1, :] = jnp.sum(part, axis=0, keepdims=True)
        inverse_ref[p : p + 1, :] = jnp.broadcast_to(inverse[:1], (1, inverse_ref.shape[1]))
        lives.append(live)
    masked_ref[...] = normed * jnp.concatenate(lives, axis=0).astype(BF16)
    pooled = pooled_ref[...]
    size = jnp.sqrt(jnp.sum(pooled * pooled, axis=-1, keepdims=True) + 1e-06)
    unit_ref[...] = (pooled / size).astype(BF16)


def slope_kernel(weight_ref, bias_ref, *refs):
    *piece_refs, slope_ref, column_ref = refs
    width = weight_ref.shape[0]
    cores = size_of("c")
    part = column_ref.shape[0] // (2 * cores)
    row = lax.broadcasted_iota(jnp.int32, (2 * cores * part, width), 0)
    source = lax.broadcasted_iota(jnp.int32, (2 * cores * part, width), 1)
    shift = row * 0
    for j in range(cores):
        for far in range(2):
            block = 2 * j + far
            half = (lax.axis_index("zh") + far) % 2
            core = (lax.axis_index("c") + j) % cores
            begin = (half * size_of("x", "c") + lax.axis_index("x") * cores + core) * part
            shift = jnp.where(row >= block * part, begin - block * part, shift)
    pick = jnp.where(source == row + shift, 1.0, 0.0).astype(BF16)
    bias = bias_ref[...].reshape(1, width)
    at = 0
    for ref in piece_refs:
        piece = ref[...]
        block = piece.shape[0]
        pre = jnp.dot(piece, weight_ref[...], preferred_element_type=F32) + bias
        square = pre * pre
        hyper = jnp.tanh(COEFF * (pre + CUBIC * pre * square))
        slope = 0.5 * (1.0 + hyper) + 0.5 * pre * (1.0 - hyper * hyper) * COEFF * (
            1.0 + 3.0 * CUBIC * square
        )
        slope_ref[at : at + block, :] = slope.astype(BF16)
        columns = lax.dot_general(pick, piece, (((1,), (1,)), ((), ())), preferred_element_type=F32)
        column_ref[:, at : at + block] = columns.astype(BF16)
        at += block


def copies_kernel(image_ref, out_ref):
    rows = image_ref.shape[1]
    for k in range(out_ref.shape[0]):
        for j in range(image_ref.shape[0]):
            out_ref[k, j * rows : (j + 1) * rows, :] = image_ref[j]


def logit_kernel(scale_ref, shift_ref, *refs):
    *unit_refs, image_ref, out_ref = refs
    near, rows, width = out_ref.shape
    group = rows * size_of("y", "za", "zb")
    units = jnp.concatenate([ref[...] for ref in unit_refs], axis=0)
    images = image_ref[...]
    temper = jnp.exp(jnp.full((1, 1), scale_ref[0], F32))
    cosine = lax.dot_general(units, images, (((1,), (1,)), ((), ())), preferred_element_type=F32)
    logit = temper * cosine + shift_ref[0]
    unit_at = lax.broadcasted_iota(jnp.int32, cosine.shape, 0)
    image_at = lax.broadcasted_iota(jnp.int32, cosine.shape, 1)
    offset = (lax.axis_index("y") * size_of("za") + lax.axis_index("za")) * rows
    label = jnp.where((unit_at == image_at - offset) & (unit_at < rows), 1.0, -1.0)
    dlogit = (-label / (1.0 + jnp.exp(label * logit)) / group).astype(BF16)
    terms = jnp.dot(dlogit, images, preferred_element_type=F32).astype(BF16)
    for k in range(near):
        owner = lax.rem(lax.axis_index("zb") + near - k, near)
        out_ref[owner] = terms[k * rows : (k + 1) * rows]


def share_kernel(scale_ref, term_ref, pooled_ref, inverse_ref, out_ref):
    temper = jnp.exp(jnp.full((1, 1), scale_ref[0], F32))
    pooled = pooled_ref[...]
    size = jnp.sqrt(jnp.sum(pooled * pooled, axis=-1, keepdims=True) + 1e-06)
    unit = pooled / size
    total = term_ref[0].astype(F32)
    for k in range(1, term_ref.shape[0]):
        total = total + term_ref[k].astype(F32)
    dunit = temper * total
    dpooled = (dunit - unit * jnp.sum(unit * dunit, axis=-1, keepdims=True)) / size
    share = (dpooled * inverse_ref[:, :1]).astype(BF16)
    for k in range(out_ref.shape[0]):
        out_ref[k] = share


def grad_kernel(share_ref, slope_ref, column_ref, keep_ref, send_ref, dpre_ref):
    along, rows, width = share_ref.shape
    block = slope_ref.shape[0] // along
    rest = keep_ref.shape[0]
    for k in range(along):
        owner = lax.rem(lax.axis_index("x") + along - k, along)
        share = share_ref[owner].astype(F32)
        share = jnp.broadcast_to(share[:, None, :], (rows, block // rows, width)).reshape(block, width)
        slope = slope_ref[k * block : (k + 1) * block, :].astype(F32)
        dpre_ref[k * block : (k + 1) * block, :] = (share * slope).astype(BF16)
    total = jnp.dot(column_ref[...], dpre_ref[...], preferred_element_type=F32)
    keep_ref[...] = total[:rest]
    send_ref[...] = total[rest:].astype(BF16)


def core_kernel(keep_ref, away_ref, near_ref, far_ref):
    total = keep_ref[...] + away_ref[...].astype(F32)
    part = near_ref.shape[0]
    near_ref[...] = total[:part]
    far_ref[...] = total[part:].astype(BF16)


def add_kernel(near_ref, away_ref, out_ref):
    out_ref[0] = near_ref[...] + away_ref[...].astype(F32)


def on_device(
    tokens, token_count, image_embed, norm_gain, head_weight, head_bias, logit_scale, logit_bias
):
    rows, length, width = tokens.shape
    part = width // size_of("zh", "x", "c")
    flat = rows * length
    total = size_of("x") * flat
    swap = [(0, 1), (1, 0)]

    (image,) = local(image_kernel, [((size_of("za"), rows, width), BF16)], image_embed)
    tokens, image = lax.optimization_barrier((tokens, image))
    some_images = exchange(image, "za")

    masked, unit, pooled, inverse = local(
        front_kernel,
        [((flat, width), BF16), ((rows, width), BF16), ((rows, width), F32), ((rows, 128), F32)],
        token_count,
        tokens.reshape(flat, width),
        norm_gain,
        head_weight,
        head_bias,
        smem=(0,),
        scratch=[((flat, width), F32)],
        flops=2 * flat * width * width,
        moved=2 * width * width,
        limit=60,
    )
    units = from_others(unit, "zb")
    by_x = from_others(masked, "x")
    mine, *middle, last = by_x
    last, units, some_images = lax.optimization_barrier((last, units, some_images))
    (copies,) = local(
        copies_kernel, [((size_of("y"), size_of("za") * rows, width), BF16)], some_images
    )
    all_images = exchange(copies, "y").reshape(-1, width)
    (terms,) = local(
        logit_kernel,
        [((size_of("zb"), rows, width), BF16)],
        logit_scale,
        logit_bias,
        *units,
        all_images,
        smem=(0, 1),
    )
    terms, middle[1:], last = lax.optimization_barrier((terms, middle[1:], last))
    by_x = [mine, *middle, last]
    terms = exchange(terms, "zb")
    slope, columns = local(
        slope_kernel,
        [((total, width), BF16), ((4 * part, total), BF16)],
        head_weight,
        head_bias,
        *by_x,
        flops=2 * total * width * width,
        moved=2 * width * width + 4 * total * width,
        limit=60,
    )
    (share,) = local(
        share_kernel,
        [((size_of("x"), rows, width), BF16)],
        logit_scale,
        terms,
        pooled,
        inverse,
        smem=(0,),
    )
    shares = exchange(share, "x")
    keep, send = local(
        grad_kernel,
        [((2 * part, width), F32), ((2 * part, width), BF16)],
        shares,
        slope,
        columns,
        scratch=[((total, width), BF16)],
        flops=8 * part * total * width,
        moved=2 * total * width,
        limit=24,
    )
    away = lax.ppermute(send, "c", swap)
    near, far = local(core_kernel, [((part, width), F32), ((part, width), BF16)], keep, away)
    away = lax.ppermute(far, "zh", swap)
    (grad,) = local(add_kernel, [((1, part, width), F32)], near, away)
    return grad


def solution(mesh):
    fine = Mesh(mesh.devices.reshape(SIZES), AXES)
    in_specs = (
        P(AXES, None, None),
        P(AXES),
        P(AXES, None),
        P(),
        P(),
        P(),
        P(),
        P(),
    )
    out_specs = P(("y", "za", "zb"), ("zh", "x", "c"), None)
    return jax.shard_map(
        on_device, mesh=fine, in_specs=in_specs, out_specs=out_specs, check_vma=False
    )
```
